128 devices in a mesh: row: 64 (over x, z, y), col: 2 (over core).
Axes of the slice: x: 4, y: 4, z: 4, core: 2. Of those that a mesh axis runs over, the one named last changes fastest.
Arguments:
- tsdf_prior: float32 [2048, 64, 256], P('row', None, 'col'), may hold values from -1 to 1
- prior_weight: float32 [2048, 64, 256], P('row', None, 'col'), may hold values from 0.5 to 8
- depth_maps: float32 [64, 131072], P('row'), may hold values from 0 to 64
- confidence: float32 [64, 131072], P('row'), may hold values from 0.2 to 5
- frustum_tiles: int32 [128, 128, 2], P(('row', 'col')), may hold values from -1 to 31, as said below
- pixel_index: int32 [128, 128, 2, 128], P(('row', 'col')), may hold values from 0 to 131071
- conv_weights: bfloat16 [3, 64, 16, 3, 3], replicated, may hold values from -0.5 to 0.5
Outputs:
- refined: float32 [2048, 64, 256], P('row', None, 'col')
- new_weight: float32 [2048, 64, 256], P('row', None, 'col')
The draws below stay inside these ranges and needn't reach their ends.
Inputs may be any that keep to these rules, and one draw needn't show every extreme that they name: `frustum_tiles`: -1 marks an empty slot; otherwise the entry is one of the owner's 32 tiles, and slot s names a tile from the s-th of 2 equal runs of tile numbers.
All inputs are finite; a program needn't handle non-finite values.
Results may differ from the reference program's by a relative error of at most 0.003.
Values may be sent and summed in bfloat16 or wider, within the bound.
No kernel may reach another device: no remote copies, remote signals or barrier semaphores. Data moves between devices by JAX's collectives and lax.ppermute only.
A program may use at most 128 MiB of HBM per device.

```python
import math
import jax
import jax.numpy as jnp
from jax import lax

HB = 64
TC = 128
GR = 32
PIX = 131072
CAP = 2
GROUPS = 4
TRUNC = 4
LAYERS = 3
READERS = 128
OWNERS = 128
MAPS = 64
NGR = 2048
NGC = 256
N_ROW = 64
N_COL = 2


def draw_frustum_tiles(key, part):
    first, second, third = jax.random.split(key, 3)
    span = GR // CAP
    layout = (READERS, OWNERS, CAP)
    within = jax.random.randint(first, layout, 0, span)
    chosen = within + span * jnp.arange(CAP, dtype=jnp.int32)
    density = jax.random.randint(second, (READERS, 1, 1), 20, 100)
    rolled = jax.random.randint(third, layout, 0, 100)
    picked = jnp.where(rolled < density, chosen, -1)
    picked = picked.at[0, 0, CAP - 1].set(GR - 1)
    picked = picked.at[0, OWNERS - 1, 0].set(-1)
    return picked.astype(jnp.int32)


def touch_ends(result, own_key, least, largest):
    dims = result.shape
    spot = [jax.random.randint(jax.random.fold_in(own_key, axis), (), 0, dims[axis]) for axis in range(len(dims))]
    result = result.at[tuple(spot)].set(least)
    longest = dims.index(max(dims))
    spot[longest] = (spot[longest] + 1) % dims[longest]
    return result.at[tuple(spot)].set(largest)


def level_of(key, shape, cuts, smallest, largest):
    gain = 1.0
    for axis_at, blocks in cuts:
        draws = jax.random.uniform(jax.random.fold_in(jax.random.fold_in(key, 6), axis_at), (blocks,), jnp.float32, smallest / len(cuts), largest / len(cuts))
        gain = gain * jnp.repeat(jnp.exp(draws), shape[axis_at] // blocks).reshape((-1,) + (1,) * (len(shape) - 1 - axis_at))
    return gain


def normal_values(key, extent, scale, reach, kind=jnp.bfloat16):
    return jnp.clip(scale * jax.random.normal(key, extent, jnp.float32), -reach, reach).astype(kind)


def setup_inputs(seed: int = 0) -> dict:
    key_list = jax.random.split(jax.random.key(seed), 8)
    tsdf_prior = jnp.clip(jax.random.uniform(key_list[0], (NGR, HB, NGC), jnp.float32, -1.0, 1.0) * level_of(key_list[0], (NGR, HB, NGC), ((0, 64), (2, 2)), -0.4, 0.0), -1.0, 1.0)
    prior_weight = jnp.clip(jnp.exp(math.log(8.0) - 2.7725887 * jax.random.uniform(key_list[1], (NGR, HB, NGC), jnp.float32) ** level_of(key_list[1], (NGR, HB, NGC), ((0, 64), (2, 2)), -0.2, 0.2)), 0.5, 8.0)
    depth_maps = jnp.clip(64.0 * jax.random.uniform(key_list[2], (MAPS, PIX), jnp.float32) ** level_of(key_list[2], (MAPS, PIX), ((0, 64),), -0.2, 0.2), 0.0, 64.0)
    confidence = jnp.clip(jnp.exp(math.log(5.0) - 3.218876 * jax.random.uniform(key_list[3], (MAPS, PIX), jnp.float32) ** level_of(key_list[3], (MAPS, PIX), ((0, 64),), -0.2, 0.2)), 0.2, 5.0)
    frustum_tiles = draw_frustum_tiles(jax.random.fold_in(key_list[7], 71), 0)
    pixel_index = touch_ends(jax.random.randint(key_list[5], (READERS, OWNERS, CAP, TC), 0, PIX), jax.random.fold_in(key_list[5], 1), 0, PIX - 1).astype(jnp.int32)
    conv_weights = normal_values(key_list[6], (LAYERS, HB, HB // GROUPS, 3, 3), (9 * HB // GROUPS) ** -0.5, 0.5)
    return {"tsdf_prior": tsdf_prior, "prior_weight": prior_weight, "depth_maps": depth_maps, "confidence": confidence, "frustum_tiles": frustum_tiles, "pixel_index": pixel_index, "conv_weights": conv_weights}


def contributions(blocks, heights, certainty):
    levels = jnp.arange(blocks.shape[-2], dtype=jnp.float32)[:, None]
    scaled = (heights[..., None, :] - levels) / TRUNC
    signed = jnp.clip(scaled, -1.0, 1.0)
    visible = jnp.clip(scaled + 2.0, 0.0, 1.0)
    mismatch = signed - blocks
    observed = certainty[..., None, :] * visible / (1.0 + 4.0 * mismatch * mismatch)
    return observed * signed, observed


def to_tiles(field):
    return field.reshape(N_ROW, GR, HB, N_COL, TC).transpose(0, 3, 1, 2, 4).reshape(N_ROW * N_COL, GR, HB, TC)


def from_tiles(tiled):
    return tiled.reshape(N_ROW, N_COL, GR, HB, TC).transpose(0, 2, 3, 1, 4).reshape(N_ROW * GR, HB, N_COL * TC)


def reference(tsdf_prior, prior_weight, depth_maps, confidence, frustum_tiles, pixel_index, conv_weights):
    tile_view = to_tiles(tsdf_prior)
    owners = jnp.arange(OWNERS, dtype=jnp.int32)[:, None]

    def one_reader(totals, reader):
        wanted = frustum_tiles[reader]
        clamped = jnp.maximum(wanted, 0).astype(jnp.int32)
        blocks = tile_view[owners, clamped]
        map_row = reader // N_COL
        places = pixel_index[reader]
        heights = jnp.take(depth_maps[map_row], places, axis=0)
        certainty = jnp.take(confidence[map_row], places, axis=0)
        weighted, observed = contributions(blocks, heights, certainty)
        present = (wanted >= 0).astype(jnp.float32)[:, :, None, None]
        sum_weighted = totals[0].at[owners, clamped].add(weighted * present)
        sum_observed = totals[1].at[owners, clamped].add(observed * present)
        return (sum_weighted, sum_observed), None

    zeros = jnp.zeros(tile_view.shape, jnp.float32)
    (sum_weighted, sum_observed), _ = lax.scan(one_reader, (zeros, zeros), jnp.arange(READERS, dtype=jnp.int32))
    total_weighted = from_tiles(sum_weighted)
    total_observed = from_tiles(sum_observed)
    joined_field = (prior_weight * tsdf_prior + total_weighted) / (prior_weight + total_observed)
    new_weight = prior_weight + total_observed
    current = joined_field
    for depth_step in range(LAYERS):
        activated = jax.nn.silu(current).astype(jnp.bfloat16)
        activated = lax.optimization_barrier(activated)
        padded = jnp.pad(activated, ((1, 1), (0, 0), (1, 1))).astype(jnp.float32)
        kernel = conv_weights[depth_step].astype(jnp.float32)
        response = lax.conv_general_dilated(padded[None], kernel, (1, 1), "VALID", dimension_numbers=("NHCW", "OIHW", "NHCW"), feature_group_count=GROUPS, precision=lax.Precision.HIGHEST)[0]
        current = current + response
    return current, new_weight
```

```python
import jax
import jax.numpy as jnp
from jax import lax
from jax.experimental import pallas as pl
from jax.experimental.pallas import tpu as pltpu
from jax.sharding import PartitionSpec as P

LANES = 128
BINS = 64
ROWS = 32
DEEP = 3
EXT = ROWS + 2 * DEEP
GROUP = 16
H_SCALE = 1023.0
C_SCALE = 13000.0
F32 = jnp.float32
BF16 = jnp.bfloat16
I32 = jnp.int32


def lookup_kernel(key_smem, key_ref, height_ref, conf_ref, out_ref, table):
    high = (height_ref[...] * H_SCALE + 0.5).astype(I32) - 32768
    low = (conf_ref[...] * C_SCALE + 0.5).astype(I32)
    table[...] = (high << 16) | low
    for block in range(key_ref.shape[0] // 8):
        index = key_ref[8 * block : 8 * block + 8, :]
        lane = index & (LANES - 1)
        line = index >> 7
        first = key_smem[8 * block, 0] >> 7
        last = key_smem[8 * block + 7, LANES - 1] >> 7

        def step(row, found):
            words = jnp.broadcast_to(table[pl.ds(row, 1), :], (8, LANES))
            taken = jnp.take_along_axis(words, lane, axis=1)
            return jnp.where(line == row, taken, found)

        out_ref[8 * block : 8 * block + 8, :] = lax.fori_loop(
            first, last + 1, step, jnp.zeros((8, LANES), I32)
        )


def lookup(keys, heights, confidence):
    return pl.pallas_call(
        lookup_kernel,
        out_shape=jax.ShapeDtypeStruct(keys.shape, I32),
        in_specs=[
            pl.BlockSpec(memory_space=pltpu.SMEM),
            pl.BlockSpec(memory_space=pltpu.VMEM),
            pl.BlockSpec(memory_space=pltpu.VMEM),
            pl.BlockSpec(memory_space=pltpu.VMEM),
        ],
        out_specs=pl.BlockSpec(memory_space=pltpu.VMEM),
        scratch_shapes=[pltpu.VMEM(heights.shape, I32)],
        compiler_params=pltpu.CompilerParams(vmem_limit_bytes=32 << 20),
        name="lookup",
    )(keys, keys, heights, confidence)


def join_kernel(
    spot_ref, list_ref, words_ref, prior_ref, weight_ref, joined_ref, new_ref, edge_ref, height, certainty
):
    col = spot_ref[1]
    word = words_ref[...]
    height[...] = ((word >> 16) + 32768).astype(F32) * (0.25 / H_SCALE)
    certainty[...] = (word & 0xFFFF).astype(F32) * (1.0 / C_SCALE)
    new_ref[...] = weight_ref[...]
    joined_ref[...] = weight_ref[...] * prior_ref[...]
    level = lax.broadcasted_iota(I32, (BINS, LANES), 0).astype(F32) * 0.25

    def term(reader, slot):
        tile = list_ref[reader, slot]
        prior = prior_ref[jnp.maximum(tile, 0)]
        scaled = height[pl.ds(2 * reader + slot, 1), :] - level
        signed = jnp.clip(scaled, -1.0, 1.0)
        visible = jnp.clip(scaled + 2.0, 0.0, 1.0)
        mismatch = signed - prior
        spread = 1.0 + 4.0 * (mismatch * mismatch)
        inverse = pl.reciprocal(spread, approx=True)
        inverse = inverse * (2.0 - spread * inverse)
        observed = (certainty[pl.ds(2 * reader + slot, 1), :] * visible) * inverse
        return tile, observed, observed * signed

    def add(tile, observed, weighted):
        @pl.when(tile >= 0)
        def _():
            new_ref[tile] += observed
            joined_ref[tile] += weighted

    def step(reader, carry):
        terms = [term(reader, slot) for slot in range(2)]
        for one in terms:
            add(*one)
        return carry

    lax.fori_loop(0, list_ref.shape[0], step, 0)
    lane = lax.broadcasted_iota(I32, (BINS, LANES), 1)
    source = jnp.where(col == 0, LANES - DEEP, 0)
    edge = jnp.zeros((BINS, LANES), F32)
    for row in range(ROWS):
        value = joined_ref[row] / new_ref[row]
        joined_ref[row] = value
        start = (row + DEEP) * DEEP
        moved = pltpu.roll(value, (start - source + LANES) % LANES, 1)
        edge = jnp.where((lane >= start) & (lane < start + DEEP), moved, edge)
    edge_ref[...] = edge


def join(spot, lists, words, prior, weight):
    tall = jax.ShapeDtypeStruct(prior.shape, F32)
    vmem = pl.BlockSpec(memory_space=pltpu.VMEM)
    smem = pl.BlockSpec(memory_space=pltpu.SMEM)
    return pl.pallas_call(
        join_kernel,
        out_shape=(tall, tall, jax.ShapeDtypeStruct((BINS, LANES), F32)),
        in_specs=[smem, smem, vmem, vmem, vmem],
        out_specs=(vmem, vmem, vmem),
        scratch_shapes=[pltpu.VMEM(words.shape, F32), pltpu.VMEM(words.shape, F32)],
        compiler_params=pltpu.CompilerParams(vmem_limit_bytes=32 << 20),
        name="join",
    )(spot, lists, words, prior, weight)


def silu(value):
    half = 0.5 * value
    return half + half * jnp.tanh(half)


def weight_matrices(taps_ref, matrix):
    layers, bins, taps = taps_ref.shape
    tap = lax.broadcasted_iota(I32, (taps, 3 * BINS), 0)
    place = lax.broadcasted_iota(I32, (taps, 3 * BINS), 1)
    out_bin = lax.broadcasted_iota(I32, (BINS, 3 * BINS), 0)
    in_bin = lax.broadcasted_iota(I32, (BINS, 3 * BINS), 1) & (BINS - 1)
    same = (out_bin // GROUP) == (in_bin // GROUP)
    wanted = (place & (GROUP - 1)) * 9 + (place // BINS) * 3
    for offset in range(3):
        chosen = (tap == wanted + offset).astype(F32).astype(BF16)
        for layer in range(layers):
            spread = jnp.dot(taps_ref[layer], chosen, preferred_element_type=F32)
            matrix[layer, BINS * offset : BINS * (offset + 1), :] = jnp.where(same, spread, 0.0).astype(BF16)


def refine_kernel(
    spot_ref, taps_ref, joined_ref, above_ref, below_ref, side_ref, out_ref, matrix, current, active, side_active
):
    row_index, col, last_row = spot_ref[0], spot_ref[1], spot_ref[2]
    weight_matrices(taps_ref, matrix)
    lane = lax.broadcasted_iota(I32, (BINS, LANES), 1)
    has_above = row_index > 0
    has_below = row_index < last_row
    inside = ((lane >= DEEP * DEEP) | has_above) & ((lane < (ROWS + DEEP) * DEEP) | has_below)
    edge_lane = jnp.where(col == 0, LANES - 1, 0)
    at_edge = lane == edge_lane
    near = jnp.where(col == 0, 0, DEEP - 1)

    side = side_ref[...]
    own = (lane >= DEEP * DEEP) & (lane < (ROWS + DEEP) * DEEP)
    side = jnp.where(own, side, 0.0)
    side = jnp.where(lane < DEEP * DEEP, pltpu.roll(above_ref[DEEP], LANES - ROWS * DEEP, 1), side)
    side = jnp.where(
        (lane >= (ROWS + DEEP) * DEEP) & (lane < EXT * DEEP), pltpu.roll(below_ref[DEEP], ROWS * DEEP, 1), side
    )
    side_current = side
    side_active[...] = jnp.where(inside, silu(side), 0.0).astype(BF16)

    for row in range(DEEP):
        current[row] = above_ref[row]
        current[ROWS + DEEP + row] = below_ref[row]
        active[0, row] = silu(above_ref[row]).astype(BF16)
        active[0, ROWS + DEEP + row] = silu(below_ref[row]).astype(BF16)

    def fill(row, carry):
        value = joined_ref[row]
        current[row + DEEP] = value
        active[0, row + DEEP] = silu(value).astype(BF16)
        return carry

    lax.fori_loop(0, ROWS, fill, 0, unroll=4)

    layers = taps_ref.shape[0]
    for layer in range(layers):
        now, later = layer % 2, (layer + 1) % 2
        taps = matrix[layer]
        inner = side_active[...].astype(F32)
        stack = jnp.concatenate(
            [pltpu.roll(inner, DEEP, 1), inner, pltpu.roll(inner, LANES - DEEP, 1)], axis=0
        ).astype(BF16)
        side_part = jnp.dot(taps, stack, preferred_element_type=F32)
        side_left, side_mid, side_right = (side_part[BINS * i : BINS * (i + 1)] for i in range(3))
        side_edge = jnp.where(col == 0, side_right, side_left)
        first = 1 + layer
        pairs = (EXT - 2 - 2 * layer) // 2
        final = layer == layers - 1

        def pair(step, injected):
            row = first + 2 * step
            planes = [active[now, row - 1 + i] for i in range(4)]
            stack = jnp.concatenate(
                [jnp.concatenate(planes[0:3], axis=0), jnp.concatenate(planes[1:4], axis=0)], axis=1
            )
            part = jnp.dot(taps, stack, preferred_element_type=F32)
            for i in range(2):
                here = row + i
                left, mid, right = (
                    part[BINS * k : BINS * (k + 1), LANES * i : LANES * (i + 1)] for k in range(3)
                )
                spot = here * DEEP + near
                moved = pltpu.roll(side_edge, (edge_lane - spot + LANES) % LANES, 1)
                response = mid + jnp.where(lane == 0, 0.0, pltpu.roll(left, 1, 1))
                response = response + jnp.where(lane == LANES - 1, 0.0, pltpu.roll(right, LANES - 1, 1))
                value = current[here] + (response + jnp.where(at_edge, moved, 0.0))
                if final:
                    out_ref[here - DEEP] = value
                else:
                    current[here] = value
                    keep = ((here >= DEEP) | has_above) & ((here < ROWS + DEEP) | has_below)
                    active[later, here] = jnp.where(keep, silu(value), 0.0).astype(BF16)
                    outward = jnp.where(col == 0, left, right)
                    thrown = pltpu.roll(outward, (spot - edge_lane + LANES) % LANES, 1)
                    injected = jnp.where(lane == spot, thrown, injected)
            return injected

        injected = lax.fori_loop(0, pairs, pair, jnp.zeros((BINS, LANES), F32))
        if not final:
            place = lane % DEEP
            from_left = jnp.where((place == 0) & (col == 0), injected, pltpu.roll(side_left, 1, 1))
            from_right = jnp.where((place == DEEP - 1) & (col != 0), injected, pltpu.roll(side_right, LANES - 1, 1))
            side_current = side_current + (side_mid + from_left + from_right)
            side_active[...] = jnp.where(inside, silu(side_current), 0.0).astype(BF16)


def refine(spot, taps, joined, above, below, side):
    vmem = pl.BlockSpec(memory_space=pltpu.VMEM)
    smem = pl.BlockSpec(memory_space=pltpu.SMEM)
    return pl.pallas_call(
        refine_kernel,
        out_shape=jax.ShapeDtypeStruct(joined.shape, F32),
        in_specs=[smem] + [vmem] * 5,
        out_specs=vmem,
        scratch_shapes=[
            pltpu.VMEM((taps.shape[0], 3 * BINS, 3 * BINS), BF16),
            pltpu.VMEM((EXT, BINS, LANES), F32),
            pltpu.VMEM((2, EXT, BINS, LANES), BF16),
            pltpu.VMEM((BINS, LANES), BF16),
        ],
        compiler_params=pltpu.CompilerParams(vmem_limit_bytes=32 << 20),
        name="refine",
    )(spot, taps, joined, above, below, side)


def on_device(tsdf_prior, prior_weight, depth_maps, confidence, frustum_tiles, pixel_index, conv_weights):
    row_count = lax.axis_size("row")
    spot = jnp.stack([lax.axis_index("row"), lax.axis_index("col"), jnp.int32(row_count - 1)]).astype(I32)
    readers = frustum_tiles.shape[1]
    pixels = pixel_index.reshape(-1)
    keys, origin = lax.sort((pixels, lax.iota(I32, pixels.shape[0])), num_keys=1, is_stable=False)
    words = lookup(
        keys.reshape(-1, LANES), depth_maps.reshape(-1, LANES), confidence.reshape(-1, LANES)
    )
    _, words = lax.sort((origin, words.reshape(-1)), num_keys=1, is_stable=False)
    lists = jnp.pad(frustum_tiles[0], ((0, 0), (0, LANES - 2)))[:, None, :]
    sent = jnp.concatenate([words.reshape(readers, 2, LANES), lists], axis=1)
    got = lax.all_to_all(sent, ("row", "col"), split_axis=0, concat_axis=0, tiled=True)
    joined, new_weight, edge = join(
        spot, got[:, 2, :2], got[:, :2, :].reshape(2 * readers, LANES), tsdf_prior, prior_weight
    )
    side = lax.ppermute(edge, "col", [(0, 1), (1, 0)])
    up = [(i, i + 1) for i in range(row_count - 1)]
    down = [(j, i) for i, j in up]
    above = lax.ppermute(jnp.concatenate([joined[ROWS - DEEP :], side[None]], axis=0), "row", up)
    below = lax.ppermute(jnp.concatenate([joined[:DEEP], side[None]], axis=0), "row", down)
    layers = conv_weights.shape[0]
    refined = refine(spot, conv_weights.reshape(layers, BINS, GROUP * 9), joined, above, below, side)
    return refined, new_weight


def solution(mesh):
    placed = (
        P("row", None, "col"),
        P("row", None, "col"),
        P("row", None),
        P("row", None),
        P(("row", "col"), None, None),
        P(("row", "col"), None, None, None),
        P(),
    )
    return jax.shard_map(
        on_device,
        mesh=mesh,
        in_specs=placed,
        out_specs=(P("row", None, "col"), P("row", None, "col")),
        check_vma=False,
    )
```

```python
import jax
import jax.numpy as jnp
from jax import lax
from jax.experimental import pallas as pl
from jax.experimental.pallas import tpu as pltpu
from jax.sharding import PartitionSpec as P

LANES = 128
BINS = 64
ROWS = 32
DEEP = 3
EXT = ROWS + 2 * DEEP
GROUP = 16
H_SCALE = 1023.0
C_SCALE = 13000.0
F32 = jnp.float32
BF16 = jnp.bfloat16
I32 = jnp.int32


def lookup_kernel(key_smem, key_ref, height_ref, conf_ref, out_ref, table):
    high = (height_ref[...] * H_SCALE + 0.5).astype(I32) - 32768
    low = (conf_ref[...] * C_SCALE + 0.5).astype(I32)
    table[...] = (high << 16) | low
    blocks = key_ref.shape[0] // 8
    chunks = table.shape[0] // 8
    together = 8

    def steps(index, carry):
        chunk, block = carry
        found = []
        for _ in range(together):
            rows = pl.ds(pl.multiple_of(block * 8, 8), 8)
            place = key_ref[rows, :]
            lane = place & (LANES - 1)
            line = place >> 7
            value = jnp.zeros((8, LANES), I32)
            for offset in range(8):
                row = chunk * 8 + offset
                words = jnp.broadcast_to(table[pl.ds(row, 1), :], (8, LANES))
                taken = jnp.take_along_axis(words, lane, axis=1)
                value = jnp.where(line == row, taken, value)
            found.append((rows, (place >> 10) == chunk, value))
            last = key_smem[8 * block + 7, LANES - 1] >> 10
            after = jnp.minimum(block + 1, blocks - 1)
            stay = last > chunk
            follow = key_smem[8 * after, 0] >> 10
            chunk = jnp.where(stay, chunk + 1, follow)
            block = jnp.where(stay, block, after)
        for rows, mine, value in found:
            out_ref[rows, :] = jnp.where(mine, value, out_ref[rows, :])
        return chunk, block

    lax.fori_loop(0, (blocks + chunks) // together, steps, (key_smem[0, 0] >> 10, jnp.int32(0)))


def lookup(keys, heights, confidence):
    return pl.pallas_call(
        lookup_kernel,
        out_shape=jax.ShapeDtypeStruct(keys.shape, I32),
        in_specs=[
            pl.BlockSpec(memory_space=pltpu.SMEM),
            pl.BlockSpec(memory_space=pltpu.VMEM),
            pl.BlockSpec(memory_space=pltpu.VMEM),
            pl.BlockSpec(memory_space=pltpu.VMEM),
        ],
        out_specs=pl.BlockSpec(memory_space=pltpu.VMEM),
        scratch_shapes=[pltpu.VMEM(heights.shape, I32)],
        compiler_params=pltpu.CompilerParams(vmem_limit_bytes=32 << 20),
        name="lookup",
    )(keys, keys, heights, confidence)


def join_kernel(
    spot_ref, list_ref, words_ref, prior_ref, weight_ref, joined_ref, new_ref, edge_ref, height, certainty
):
    col = spot_ref[1]
    word = words_ref[...]
    height[...] = ((word >> 16) + 32768).astype(F32) * (0.25 / H_SCALE)
    certainty[...] = (word & 0xFFFF).astype(F32) * (1.0 / C_SCALE)
    new_ref[...] = weight_ref[...]
    joined_ref[...] = weight_ref[...] * prior_ref[...]
    level = lax.broadcasted_iota(I32, (BINS, LANES), 0).astype(F32) * 0.25

    def term(reader, slot):
        tile = list_ref[reader, slot]
        prior = prior_ref[jnp.maximum(tile, 0)]
        scaled = height[pl.ds(2 * reader + slot, 1), :] - level
        signed = jnp.clip(scaled, -1.0, 1.0)
        visible = jnp.clip(scaled + 2.0, 0.0, 1.0)
        mismatch = signed - prior
        spread = 1.0 + 4.0 * (mismatch * mismatch)
        inverse = pl.reciprocal(spread, approx=True)
        inverse = inverse * (2.0 - spread * inverse)
        observed = (certainty[pl.ds(2 * reader + slot, 1), :] * visible) * inverse
        return tile, observed, observed * signed

    def add(tile, observed, weighted):
        @pl.when(tile >= 0)
        def _():
            new_ref[tile] += observed
            joined_ref[tile] += weighted

    def step(reader, carry):
        terms = [term(reader, slot) for slot in range(2)]
        for one in terms:
            add(*one)
        return carry

    lax.fori_loop(0, list_ref.shape[0], step, 0)
    lane = lax.broadcasted_iota(I32, (BINS, LANES), 1)
    source = jnp.where(col == 0, LANES - DEEP, 0)
    edge = jnp.zeros((BINS, LANES), F32)
    for row in range(ROWS):
        value = joined_ref[row] / new_ref[row]
        joined_ref[row] = value
        start = (row + DEEP) * DEEP
        moved = pltpu.roll(value, (start - source + LANES) % LANES, 1)
        edge = jnp.where((lane >= start) & (lane < start + DEEP), moved, edge)
    edge_ref[...] = edge


def join(spot, lists, words, prior, weight):
    tall = jax.ShapeDtypeStruct(prior.shape, F32)
    vmem = pl.BlockSpec(memory_space=pltpu.VMEM)
    smem = pl.BlockSpec(memory_space=pltpu.SMEM)
    return pl.pallas_call(
        join_kernel,
        out_shape=(tall, tall, jax.ShapeDtypeStruct((BINS, LANES), F32)),
        in_specs=[smem, smem, vmem, vmem, vmem],
        out_specs=(vmem, vmem, vmem),
        scratch_shapes=[pltpu.VMEM(words.shape, F32), pltpu.VMEM(words.shape, F32)],
        compiler_params=pltpu.CompilerParams(vmem_limit_bytes=32 << 20),
        name="join",
    )(spot, lists, words, prior, weight)


def silu(value):
    half = 0.5 * value
    return half + half * jnp.tanh(half)


def weight_matrices(taps_ref, matrix):
    layers, bins, taps = taps_ref.shape
    tap = lax.broadcasted_iota(I32, (taps, 3 * BINS), 0)
    place = lax.broadcasted_iota(I32, (taps, 3 * BINS), 1)
    out_bin = lax.broadcasted_iota(I32, (BINS, 3 * BINS), 0)
    in_bin = lax.broadcasted_iota(I32, (BINS, 3 * BINS), 1) & (BINS - 1)
    same = (out_bin // GROUP) == (in_bin // GROUP)
    wanted = (place & (GROUP - 1)) * 9 + (place // BINS) * 3
    for offset in range(3):
        chosen = (tap == wanted + offset).astype(F32).astype(BF16)
        for layer in range(layers):
            spread = jnp.dot(taps_ref[layer], chosen, preferred_element_type=F32)
            matrix[layer, BINS * offset : BINS * (offset + 1), :] = jnp.where(same, spread, 0.0).astype(BF16)


def refine_kernel(
    spot_ref, taps_ref, joined_ref, above_ref, below_ref, side_ref, out_ref, matrix, current, active, side_active
):
    row_index, col, last_row = spot_ref[0], spot_ref[1], spot_ref[2]
    weight_matrices(taps_ref, matrix)
    lane = lax.broadcasted_iota(I32, (BINS, LANES), 1)
    has_above = row_index > 0
    has_below = row_index < last_row
    inside = ((lane >= DEEP * DEEP) | has_above) & ((lane < (ROWS + DEEP) * DEEP) | has_below)
    edge_lane = jnp.where(col == 0, LANES - 1, 0)
    at_edge = lane == edge_lane
    near = jnp.where(col == 0, 0, DEEP - 1)

    side = side_ref[...]
    own = (lane >= DEEP * DEEP) & (lane < (ROWS + DEEP) * DEEP)
    side = jnp.where(own, side, 0.0)
    side = jnp.where(lane < DEEP * DEEP, pltpu.roll(above_ref[DEEP], LANES - ROWS * DEEP, 1), side)
    side = jnp.where(
        (lane >= (ROWS + DEEP) * DEEP) & (lane < EXT * DEEP), pltpu.roll(below_ref[DEEP], ROWS * DEEP, 1), side
    )
    side_current = side
    side_active[...] = jnp.where(inside, silu(side), 0.0).astype(BF16)

    for row in range(DEEP):
        current[row] = above_ref[row]
        current[ROWS + DEEP + row] = below_ref[row]
        active[0, row] = silu(above_ref[row]).astype(BF16)
        active[0, ROWS + DEEP + row] = silu(below_ref[row]).astype(BF16)

    def fill(row, carry):
        value = joined_ref[row]
        current[row + DEEP] = value
        active[0, row + DEEP] = silu(value).astype(BF16)
        return carry

    lax.fori_loop(0, ROWS, fill, 0, unroll=4)

    layers = taps_ref.shape[0]
    for layer in range(layers):
        now, later = layer % 2, (layer + 1) % 2
        taps = matrix[layer]
        inner = side_active[...].astype(F32)
        stack = jnp.concatenate(
            [pltpu.roll(inner, DEEP, 1), inner, pltpu.roll(inner, LANES - DEEP, 1)], axis=0
        ).astype(BF16)
        side_part = jnp.dot(taps, stack, preferred_element_type=F32)
        side_left, side_mid, side_right = (side_part[BINS * i : BINS * (i + 1)] for i in range(3))
        side_edge = jnp.where(col == 0, side_right, side_left)
        first = 1 + layer
        pairs = (EXT - 2 - 2 * layer) // 2
        final = layer == layers - 1

        def pair(step, injected):
            row = first + 2 * step
            planes = [active[now, row - 1 + i] for i in range(4)]
            stack = jnp.concatenate(
                [jnp.concatenate(planes[0:3], axis=0), jnp.concatenate(planes[1:4], axis=0)], axis=1
            )
            part = jnp.dot(taps, stack, preferred_element_type=F32)
            for i in range(2):
                here = row + i
                left, mid, right = (
                    part[BINS * k : BINS * (k + 1), LANES * i : LANES * (i + 1)] for k in range(3)
                )
                spot = here * DEEP + near
                moved = pltpu.roll(side_edge, (edge_lane - spot + LANES) % LANES, 1)
                response = mid + jnp.where(lane == 0, 0.0, pltpu.roll(left, 1, 1))
                response = response + jnp.where(lane == LANES - 1, 0.0, pltpu.roll(right, LANES - 1, 1))
                value = current[here] + (response + jnp.where(at_edge, moved, 0.0))
                if final:
                    out_ref[here - DEEP] = value
                else:
                    current[here] = value
                    keep = ((here >= DEEP) | has_above) & ((here < ROWS + DEEP) | has_below)
                    active[later, here] = jnp.where(keep, silu(value), 0.0).astype(BF16)
                    outward = jnp.where(col == 0, left, right)
                    thrown = pltpu.roll(outward, (spot - edge_lane + LANES) % LANES, 1)
                    injected = jnp.where(lane == spot, thrown, injected)
            return injected

        injected = lax.fori_loop(0, pairs, pair, jnp.zeros((BINS, LANES), F32))
        if not final:
            place = lane % DEEP
            from_left = jnp.where((place == 0) & (col == 0), injected, pltpu.roll(side_left, 1, 1))
            from_right = jnp.where((place == DEEP - 1) & (col != 0), injected, pltpu.roll(side_right, LANES - 1, 1))
            side_current = side_current + (side_mid + from_left + from_right)
            side_active[...] = jnp.where(inside, silu(side_current), 0.0).astype(BF16)


def refine(spot, taps, joined, above, below, side):
    vmem = pl.BlockSpec(memory_space=pltpu.VMEM)
    smem = pl.BlockSpec(memory_space=pltpu.SMEM)
    return pl.pallas_call(
        refine_kernel,
        out_shape=jax.ShapeDtypeStruct(joined.shape, F32),
        in_specs=[smem] + [vmem] * 5,
        out_specs=vmem,
        scratch_shapes=[
            pltpu.VMEM((taps.shape[0], 3 * BINS, 3 * BINS), BF16),
            pltpu.VMEM((EXT, BINS, LANES), F32),
            pltpu.VMEM((2, EXT, BINS, LANES), BF16),
            pltpu.VMEM((BINS, LANES), BF16),
        ],
        compiler_params=pltpu.CompilerParams(vmem_limit_bytes=32 << 20),
        name="refine",
    )(spot, taps, joined, above, below, side)


def on_device(tsdf_prior, prior_weight, depth_maps, confidence, frustum_tiles, pixel_index, conv_weights):
    row_count = lax.axis_size("row")
    spot = jnp.stack([lax.axis_index("row"), lax.axis_index("col"), jnp.int32(row_count - 1)]).astype(I32)
    readers = frustum_tiles.shape[1]
    pixels = pixel_index.reshape(-1)
    keys, origin = lax.sort((pixels, lax.iota(I32, pixels.shape[0])), num_keys=1, is_stable=False)
    words = lookup(
        keys.reshape(-1, LANES), depth_maps.reshape(-1, LANES), confidence.reshape(-1, LANES)
    )
    _, words = lax.sort((origin, words.reshape(-1)), num_keys=1, is_stable=False)
    lists = jnp.pad(frustum_tiles[0], ((0, 0), (0, LANES - 2)))[:, None, :]
    sent = jnp.concatenate([words.reshape(readers, 2, LANES), lists], axis=1)
    got = lax.all_to_all(sent, ("row", "col"), split_axis=0, concat_axis=0, tiled=True)
    joined, new_weight, edge = join(
        spot, got[:, 2, :2], got[:, :2, :].reshape(2 * readers, LANES), tsdf_prior, prior_weight
    )
    side = lax.ppermute(edge, "col", [(0, 1), (1, 0)])
    up = [(i, i + 1) for i in range(row_count - 1)]
    down = [(j, i) for i, j in up]
    above = lax.ppermute(jnp.concatenate([joined[ROWS - DEEP :], side[None]], axis=0), "row", up)
    below = lax.ppermute(jnp.concatenate([joined[:DEEP], side[None]], axis=0), "row", down)
    layers = conv_weights.shape[0]
    refined = refine(spot, conv_weights.reshape(layers, BINS, GROUP * 9), joined, above, below, side)
    return refined, new_weight


def solution(mesh):
    placed = (
        P("row", None, "col"),
        P("row", None, "col"),
        P("row", None),
        P("row", None),
        P(("row", "col"), None, None),
        P(("row", "col"), None, None, None),
        P(),
    )
    return jax.shard_map(
        on_device,
        mesh=mesh,
        in_specs=placed,
        out_specs=(P("row", None, "col"), P("row", None, "col")),
        check_vma=False,
    )
```

```python
import jax
import jax.numpy as jnp
from jax import lax
from jax.experimental import pallas as pl
from jax.experimental.pallas import tpu as pltpu
from jax.sharding import PartitionSpec as P

LANES = 128
BINS = 64
ROWS = 32
DEEP = 3
EXT = ROWS + 2 * DEEP
GROUP = 16
TOGETHER = 18
AT_ONCE = 4
H_SCALE = 1023.0
C_SCALE = 13000.0
F32 = jnp.float32
BF16 = jnp.bfloat16
I32 = jnp.int32


BY_BLOCK = [("v", 0), ("v", 1), ("v", 2), ("v", 3), ("s", 0), ("s", 1), ("s", 2), ("l", 0), ("l", 1), ("l", 2)]
BY_BLOCK += [("v", 4), ("l", 3), ("l", 4), ("l", 5), ("l", 6)]
BY_LANE = [("v", i) for i in range(5)] + [("s", i) for i in range(3)] + [("l", i) for i in range(7)]
REGISTERS = 32
LAG = 8


def along(kind):
    return lax.broadcasted_iota(I32, (8, LANES), 0 if kind == "s" else 1)


def exchange(parts, kind, bit):
    distance = 1 << bit
    if kind == "v":
        parts = list(parts)
        for low in range(REGISTERS):
            if low & distance == 0:
                one, two = parts[low], parts[low | distance]
                parts[low], parts[low | distance] = jnp.minimum(one, two), jnp.maximum(one, two)
        return parts
    axis = 0 if kind == "s" else 1
    size = (8, LANES)[axis]
    upper = (along(kind) & distance) != 0
    result = []
    for part in parts:
        from_low = pltpu.roll(part, distance, axis)
        from_high = from_low if 2 * distance == size else pltpu.roll(part, size - distance, axis)
        result.append(jnp.where(upper, jnp.maximum(part, from_low), jnp.minimum(part, from_high)))
    return result


def turn(parts, places):
    fixed = [bit for kind, bit in places if kind == "v"]
    mask = None
    for kind, bit in places:
        if kind != "v":
            one = -((along(kind) >> bit) & 1)
            mask = one if mask is None else mask ^ one
    result = []
    for register, part in enumerate(parts):
        if sum((register >> bit) & 1 for bit in fixed) % 2:
            part = ~part
        result.append(part if mask is None else part ^ mask)
    return result


def sort_steps(order):
    size = len(order)
    for phase in range(1, size + 1):
        yield "turn", [order[place] for place in (phase - 1, phase) if 0 < place < size and phase + place > 1]
        for place in range(phase - 1, -1, -1):
            yield "exchange", order[place]


def advance(parts, step):
    kind, what = step
    return turn(parts, what) if kind == "turn" else exchange(parts, *what)


def sample_kernel(pixel_ref, wanted_ref, height_hbm, conf_hbm, out_ref, maps, table, blocks, found, edges, bounds, sems):
    copies = [
        pltpu.make_async_copy(height_hbm, maps.at[0], sems.at[0]),
        pltpu.make_async_copy(conf_hbm, maps.at[1], sems.at[1]),
    ]
    for copy in copies:
        copy.start()
    parts = []
    for register in range(REGISTERS):
        pixel = pixel_ref[8 * register : 8 * register + 8, :]
        place = ((along("s") & 1) << 4) + (register >> 1)
        place = place + ((4 * (register & 1) + (along("s") >> 1)) << 5) + (along("l") << 8)
        parts.append(((pixel - 65536) << 15) | place)
    for step in sort_steps(BY_BLOCK):
        parts = advance(parts, step)
    for i, register in enumerate((0, 16, 15, 31)):
        edges[8 * i : 8 * i + 8, :] = parts[register]
    to_scalar = pltpu.make_async_copy(edges, bounds, sems.at[2])
    to_scalar.start()
    for half in range(2):
        turned = jnp.concatenate(parts[16 * half : 16 * half + 16], axis=0).T
        for i in range(16):
            blocks[8 * (2 * i + half) : 8 * (2 * i + half) + 8, :] = turned[8 * i : 8 * i + 8, :]
    for copy in copies:
        copy.wait()
    high = (maps[0] * H_SCALE + 0.5).astype(I32) - 32768
    low = (maps[1] * C_SCALE + 0.5).astype(I32)
    table[...] = (high << 16) | low
    to_scalar.wait()
    chunks = table.shape[0] // 8
    together = 8

    def first_chunk(block):
        return (bounds[8 * (block & 1), 8 * (block >> 1)] >> 25) + 64

    def last_chunk(block):
        return (bounds[23 + 8 * (block & 1), 8 * (block >> 1) + 7] >> 25) + 64

    def walk(index, carry):
        chunk, block = carry
        pending = []
        for _ in range(together):
            rows = pl.ds(pl.multiple_of(block * 8, 8), 8)
            key = blocks[rows, :]
            lane = (key >> 15) & (LANES - 1)
            line = (key >> 22) + 512
            value = jnp.zeros((8, LANES), I32)
            for offset in range(8):
                row = chunk * 8 + offset
                words = jnp.broadcast_to(table[pl.ds(row, 1), :], (8, LANES))
                taken = jnp.take_along_axis(words, lane, axis=1)
                value = jnp.where(line == row, taken, value)
            pending.append((rows, (line >> 3) == chunk, value))
            after = jnp.minimum(block + 1, REGISTERS - 1)
            stay = last_chunk(block) > chunk
            chunk = jnp.where(stay, chunk + 1, first_chunk(after))
            block = jnp.where(stay, block, after)
        for rows, mine, value in pending:
            found[rows, :] = jnp.where(mine, value, found[rows, :])
        return chunk, block

    lax.fori_loop(0, (REGISTERS + chunks) // together, walk, (first_chunk(0), jnp.int32(0)))
    highs, lows = [], []
    for register in range(REGISTERS):
        rows = slice(8 * register, 8 * register + 8)
        place = ((blocks[rows, :] & 32767) - 16384) << 16
        word = found[rows, :]
        highs.append(place | ((word >> 16) & 0xFFFF))
        lows.append(place | (word & 0xFFFF))
    steps = list(sort_steps(BY_LANE))
    for i in range(len(steps) + LAG):
        if i < len(steps):
            highs = advance(highs, steps[i])
        if i >= LAG:
            lows = advance(lows, steps[i - LAG])
    for register in range(REGISTERS):
        slot, owner = register >> 4, 8 * (register & 15)
        out_ref[pl.ds(3 * owner + slot, 8, stride=3), :] = (highs[register] << 16) | (lows[register] & 0xFFFF)
    wanted = jnp.concatenate([wanted_ref[...], jnp.zeros((LANES - 2, LANES), I32)], axis=0).T
    for owner in range(0, LANES, 8):
        out_ref[pl.ds(3 * owner + 2, 8, stride=3), :] = wanted[owner : owner + 8, :]


def sample(pixels, wanted, heights, confidence):
    flat = pltpu.VMEM(pixels.shape, I32)
    return pl.pallas_call(
        sample_kernel,
        out_shape=jax.ShapeDtypeStruct((3 * wanted.shape[1], LANES), I32),
        in_specs=[
            pl.BlockSpec(memory_space=pltpu.VMEM),
            pl.BlockSpec(memory_space=pltpu.VMEM),
            pl.BlockSpec(memory_space=pl.ANY),
            pl.BlockSpec(memory_space=pl.ANY),
        ],
        out_specs=pl.BlockSpec(memory_space=pltpu.VMEM),
        scratch_shapes=[
            pltpu.VMEM((2,) + heights.shape, F32),
            pltpu.VMEM(heights.shape, I32),
            flat,
            flat,
            pltpu.VMEM((32, LANES), I32),
            pltpu.SMEM((32, LANES), I32),
            pltpu.SemaphoreType.DMA((3,)),
        ],
        compiler_params=pltpu.CompilerParams(vmem_limit_bytes=60 << 20),
        name="sample",
    )(pixels, wanted, heights, confidence)


def join_kernel(
    spot_ref, list_ref, words_ref, prior_ref, weight_ref, joined_ref, new_ref, edge_ref, order_ref, height, certainty
):
    col = spot_ref[1]
    entries = words_ref.shape[0]
    word = words_ref[...]
    height[0:entries, :] = ((word >> 16) + 32768).astype(F32) * (0.5 / H_SCALE)
    certainty[0:entries, :] = (word & 0xFFFF).astype(F32) * (0.5 / C_SCALE)
    height[entries:, :] = jnp.zeros((8, LANES), F32)
    certainty[entries:, :] = jnp.zeros((8, LANES), F32)
    new_ref[...] = weight_ref[...]
    joined_ref[...] = (2.0 * weight_ref[...]) * prior_ref[...]
    level = lax.broadcasted_iota(I32, (BINS, LANES), 0).astype(F32) * 0.5

    def pick(reader, count):
        for slot in range(2):
            tile = list_ref[reader, slot]
            order_ref[count] = tile * 512 + (3 * reader + slot)
            count = count + jnp.where(tile >= 0, 1, 0)
        return count

    count = lax.fori_loop(0, list_ref.shape[0], pick, jnp.int32(0), unroll=4)
    for i in range(AT_ONCE):
        order_ref[count + i] = entries

    def term(place):
        code = order_ref[place]
        tile = code >> 9
        entry = code & 511
        prior = prior_ref[tile]
        scaled = height[pl.ds(entry, 1), :] - level
        signed = jnp.clip(scaled, -2.0, 2.0)
        visible = jnp.clip(scaled + 4.0, 0.0, 2.0)
        mismatch = signed - (prior + prior)
        spread = 1.0 + mismatch * mismatch
        inverse = pl.reciprocal(spread, approx=True)
        inverse = inverse * (2.0 - spread * inverse)
        observed = (certainty[pl.ds(entry, 1), :] * visible) * inverse
        return tile, observed, observed * signed

    def step(index, carry):
        terms = [term(AT_ONCE * index + i) for i in range(AT_ONCE)]
        for tile, observed, weighted in terms:
            new_ref[tile] += observed
            joined_ref[tile] += weighted
        return carry

    lax.fori_loop(0, (count + AT_ONCE - 1) // AT_ONCE, step, 0)
    lane = lax.broadcasted_iota(I32, (BINS, LANES), 1)
    source = jnp.where(col == 0, LANES - DEEP, 0)
    edge = jnp.zeros((BINS, LANES), F32)
    for row in range(ROWS):
        value = (0.5 * joined_ref[row]) / new_ref[row]
        joined_ref[row] = value
        start = (row + DEEP) * DEEP
        moved = pltpu.roll(value, (start - source + LANES) % LANES, 1)
        edge = jnp.where((lane >= start) & (lane < start + DEEP), moved, edge)
    edge_ref[...] = edge


def join(spot, lists, words, prior, weight):
    tall = jax.ShapeDtypeStruct(prior.shape, F32)
    vmem = pl.BlockSpec(memory_space=pltpu.VMEM)
    smem = pl.BlockSpec(memory_space=pltpu.SMEM)
    return pl.pallas_call(
        join_kernel,
        out_shape=(tall, tall, jax.ShapeDtypeStruct((BINS, LANES), F32)),
        in_specs=[smem, smem, vmem, vmem, vmem],
        out_specs=(vmem, vmem, vmem),
        scratch_shapes=[pltpu.SMEM((2 * lists.shape[0] + AT_ONCE,), I32)]
        + [pltpu.VMEM((words.shape[0] + 8, LANES), F32)] * 2,
        compiler_params=pltpu.CompilerParams(vmem_limit_bytes=32 << 20),
        name="join",
    )(spot, lists, words, prior, weight)


def silu(value):
    half = 0.5 * value
    return half + half * jnp.tanh(half)


def weight_matrices(taps_ref, matrix):
    layers, bins, taps = taps_ref.shape
    tap = lax.broadcasted_iota(I32, (taps, 3 * BINS), 0)
    place = lax.broadcasted_iota(I32, (taps, 3 * BINS), 1)
    out_bin = lax.broadcasted_iota(I32, (BINS, 3 * BINS), 0)
    in_bin = lax.broadcasted_iota(I32, (BINS, 3 * BINS), 1) & (BINS - 1)
    same = (out_bin // GROUP) == (in_bin // GROUP)
    wanted = (place & (GROUP - 1)) * 9 + (place // BINS) * 3
    for offset in range(3):
        chosen = (tap == wanted + offset).astype(F32).astype(BF16)
        for layer in range(layers):
            spread = jnp.dot(taps_ref[layer], chosen, preferred_element_type=F32)
            matrix[layer, BINS * offset : BINS * (offset + 1), :] = jnp.where(same, spread, 0.0).astype(BF16)


def refine_kernel(
    spot_ref, taps_ref, joined_ref, above_ref, below_ref, side_ref, out_ref, matrix, current, active, side_active
):
    row_index, col, last_row = spot_ref[0], spot_ref[1], spot_ref[2]
    weight_matrices(taps_ref, matrix)
    lane = lax.broadcasted_iota(I32, (BINS, LANES), 1)
    has_above = row_index > 0
    has_below = row_index < last_row
    inside = ((lane >= DEEP * DEEP) | has_above) & ((lane < (ROWS + DEEP) * DEEP) | has_below)
    edge_lane = jnp.where(col == 0, LANES - 1, 0)
    at_edge = lane == edge_lane
    near = jnp.where(col == 0, 0, DEEP - 1)

    side = side_ref[...]
    own = (lane >= DEEP * DEEP) & (lane < (ROWS + DEEP) * DEEP)
    side = jnp.where(own, side, 0.0)
    side = jnp.where(lane < DEEP * DEEP, pltpu.roll(above_ref[DEEP], LANES - ROWS * DEEP, 1), side)
    side = jnp.where(
        (lane >= (ROWS + DEEP) * DEEP) & (lane < EXT * DEEP), pltpu.roll(below_ref[DEEP], ROWS * DEEP, 1), side
    )
    side_current = side
    side_active[...] = jnp.where(inside, silu(side), 0.0).astype(BF16)

    for row in range(DEEP):
        current[row] = above_ref[row]
        current[ROWS + DEEP + row] = below_ref[row]
        active[0, row] = silu(above_ref[row]).astype(BF16)
        active[0, ROWS + DEEP + row] = silu(below_ref[row]).astype(BF16)

    def fill(row, carry):
        value = joined_ref[row]
        current[row + DEEP] = value
        active[0, row + DEEP] = silu(value).astype(BF16)
        return carry

    lax.fori_loop(0, ROWS, fill, 0, unroll=4)

    layers = taps_ref.shape[0]
    for layer in range(layers):
        now, later = layer % 2, (layer + 1) % 2
        taps = matrix[layer]
        inner = side_active[...].astype(F32)
        stack = jnp.concatenate(
            [pltpu.roll(inner, DEEP, 1), inner, pltpu.roll(inner, LANES - DEEP, 1)], axis=0
        ).astype(BF16)
        side_part = jnp.dot(taps, stack, preferred_element_type=F32)
        side_left, side_mid, side_right = (side_part[BINS * i : BINS * (i + 1)] for i in range(3))
        side_edge = jnp.where(col == 0, side_right, side_left)
        first = 1 + layer
        pairs = (EXT - 2 - 2 * layer) // 2
        final = layer == layers - 1

        def pair(step, injected):
            row = first + 2 * step
            planes = [active[now, row - 1 + i] for i in range(4)]
            stack = jnp.concatenate(
                [jnp.concatenate(planes[0:3], axis=0), jnp.concatenate(planes[1:4], axis=0)], axis=1
            )
            part = jnp.dot(taps, stack, preferred_element_type=F32)
            for i in range(2):
                here = row + i
                left, mid, right = (
                    part[BINS * k : BINS * (k + 1), LANES * i : LANES * (i + 1)] for k in range(3)
                )
                spot = here * DEEP + near
                moved = pltpu.roll(side_edge, (edge_lane - spot + LANES) % LANES, 1)
                response = mid + jnp.where(lane == 0, 0.0, pltpu.roll(left, 1, 1))
                response = response + jnp.where(lane == LANES - 1, 0.0, pltpu.roll(right, LANES - 1, 1))
                value = current[here] + (response + jnp.where(at_edge, moved, 0.0))
                if final:
                    out_ref[here - DEEP] = value
                else:
                    current[here] = value
                    keep = ((here >= DEEP) | has_above) & ((here < ROWS + DEEP) | has_below)
                    active[later, here] = jnp.where(keep, silu(value), 0.0).astype(BF16)
                    outward = jnp.where(col == 0, left, right)
                    thrown = pltpu.roll(outward, (spot - edge_lane + LANES) % LANES, 1)
                    injected = jnp.where(lane == spot, thrown, injected)
            return injected

        def several(step, injected):
            for i in range(TOGETHER):
                injected = pair(TOGETHER * step + i, injected)
            return injected

        full = pairs // TOGETHER
        injected = lax.fori_loop(0, full, several, jnp.zeros((BINS, LANES), F32))
        for step in range(full * TOGETHER, pairs):
            injected = pair(step, injected)
        if not final:
            place = lane % DEEP
            from_left = jnp.where((place == 0) & (col == 0), injected, pltpu.roll(side_left, 1, 1))
            from_right = jnp.where((place == DEEP - 1) & (col != 0), injected, pltpu.roll(side_right, LANES - 1, 1))
            side_current = side_current + (side_mid + from_left + from_right)
            side_active[...] = jnp.where(inside, silu(side_current), 0.0).astype(BF16)


def refine(spot, taps, joined, above, below, side):
    vmem = pl.BlockSpec(memory_space=pltpu.VMEM)
    smem = pl.BlockSpec(memory_space=pltpu.SMEM)
    return pl.pallas_call(
        refine_kernel,
        out_shape=jax.ShapeDtypeStruct(joined.shape, F32),
        in_specs=[smem] + [vmem] * 5,
        out_specs=vmem,
        scratch_shapes=[
            pltpu.VMEM((taps.shape[0], 3 * BINS, 3 * BINS), BF16),
            pltpu.VMEM((EXT, BINS, LANES), F32),
            pltpu.VMEM((2, EXT, BINS, LANES), BF16),
            pltpu.VMEM((BINS, LANES), BF16),
        ],
        compiler_params=pltpu.CompilerParams(vmem_limit_bytes=32 << 20),
        name="refine",
    )(spot, taps, joined, above, below, side)


def on_device(tsdf_prior, prior_weight, depth_maps, confidence, frustum_tiles, pixel_index, conv_weights):
    row_count = lax.axis_size("row")
    spot = jnp.stack([lax.axis_index("row"), lax.axis_index("col"), jnp.int32(row_count - 1)]).astype(I32)
    readers = frustum_tiles.shape[1]
    both = ("row", "col")
    words = sample(
        pixel_index.reshape(-1, LANES),
        frustum_tiles[0].T,
        depth_maps.reshape(-1, LANES),
        confidence.reshape(-1, LANES),
    )
    got = lax.all_to_all(words.reshape(readers, 1, 3 * LANES), both, split_axis=0, concat_axis=0, tiled=True)
    joined, new_weight, edge = join(
        spot, got[:, 0, 2 * LANES : 2 * LANES + 2], got.reshape(3 * readers, LANES), tsdf_prior, prior_weight
    )
    side = lax.ppermute(edge, "col", [(0, 1), (1, 0)])
    up = [(i, i + 1) for i in range(row_count - 1)]
    down = [(j, i) for i, j in up]
    above = lax.ppermute(jnp.concatenate([joined[ROWS - DEEP :], side[None]], axis=0), "row", up)
    below = lax.ppermute(jnp.concatenate([joined[:DEEP], side[None]], axis=0), "row", down)
    layers = conv_weights.shape[0]
    refined = refine(spot, conv_weights.reshape(layers, BINS, GROUP * 9), joined, above, below, side)
    return refined, new_weight


def solution(mesh):
    placed = (
        P("row", None, "col"),
        P("row", None, "col"),
        P("row", None),
        P("row", None),
        P(("row", "col"), None, None),
        P(("row", "col"), None, None, None),
        P(),
    )
    return jax.shard_map(
        on_device,
        mesh=mesh,
        in_specs=placed,
        out_specs=(P("row", None, "col"), P("row", None, "col")),
        check_vma=False,
    )
```

```python
import jax
import jax.numpy as jnp
from jax import lax
from jax.experimental import pallas as pl
from jax.experimental.pallas import tpu as pltpu
from jax.sharding import PartitionSpec as P

LANES = 128
BINS = 64
ROWS = 32
DEEP = 3
EXT = ROWS + 2 * DEEP
GROUP = 16
TOGETHER = 18
AT_ONCE = 4
WIDTH = 5
JOIN_VMEM = 16
H_SCALE = 1023.0
C_SCALE = 13000.0
F32 = jnp.float32
BF16 = jnp.bfloat16
I32 = jnp.int32


BY_BLOCK = [("v", 0), ("v", 1), ("v", 2), ("v", 3), ("s", 0), ("s", 1), ("s", 2), ("l", 0), ("l", 1), ("l", 2)]
BY_BLOCK += [("v", 4), ("l", 3), ("l", 4), ("l", 5), ("l", 6)]
BY_LANE = [("v", i) for i in range(5)] + [("s", i) for i in range(3)] + [("l", i) for i in range(7)]
REGISTERS = 32
LAG = 8


def along(kind):
    return lax.broadcasted_iota(I32, (8, LANES), 0 if kind == "s" else 1)


def exchange(parts, kind, bit):
    distance = 1 << bit
    if kind == "v":
        parts = list(parts)
        for low in range(REGISTERS):
            if low & distance == 0:
                one, two = parts[low], parts[low | distance]
                parts[low], parts[low | distance] = jnp.minimum(one, two), jnp.maximum(one, two)
        return parts
    axis = 0 if kind == "s" else 1
    size = (8, LANES)[axis]
    upper = (along(kind) & distance) != 0
    result = []
    for part in parts:
        from_low = pltpu.roll(part, distance, axis)
        from_high = from_low if 2 * distance == size else pltpu.roll(part, size - distance, axis)
        result.append(jnp.where(upper, jnp.maximum(part, from_low), jnp.minimum(part, from_high)))
    return result


def turn(parts, places):
    fixed = [bit for kind, bit in places if kind == "v"]
    mask = None
    for kind, bit in places:
        if kind != "v":
            one = -((along(kind) >> bit) & 1)
            mask = one if mask is None else mask ^ one
    result = []
    for register, part in enumerate(parts):
        if sum((register >> bit) & 1 for bit in fixed) % 2:
            part = ~part
        result.append(part if mask is None else part ^ mask)
    return result


def sort_steps(order):
    size = len(order)
    for phase in range(1, size + 1):
        yield "turn", [order[place] for place in (phase - 1, phase) if 0 < place < size and phase + place > 1]
        for place in range(phase - 1, -1, -1):
            yield "exchange", order[place]


def advance(parts, step):
    kind, what = step
    return turn(parts, what) if kind == "turn" else exchange(parts, *what)


def sample_kernel(pixel_ref, wanted_ref, height_hbm, conf_hbm, out_ref, maps, table, blocks, found, edges, bounds, sems):
    copies = [
        pltpu.make_async_copy(height_hbm, maps.at[0], sems.at[0]),
        pltpu.make_async_copy(conf_hbm, maps.at[1], sems.at[1]),
    ]
    for copy in copies:
        copy.start()
    parts = []
    for register in range(REGISTERS):
        pixel = pixel_ref[8 * register : 8 * register + 8, :]
        place = ((along("s") & 1) << 4) + (register >> 1)
        place = place + ((4 * (register & 1) + (along("s") >> 1)) << 5) + (along("l") << 8)
        parts.append(((pixel - 65536) << 15) | place)
    for step in sort_steps(BY_BLOCK):
        parts = advance(parts, step)
    for i, register in enumerate((0, 16, 15, 31)):
        edges[8 * i : 8 * i + 8, :] = parts[register]
    to_scalar = pltpu.make_async_copy(edges, bounds, sems.at[2])
    to_scalar.start()
    for half in range(2):
        turned = jnp.concatenate(parts[16 * half : 16 * half + 16], axis=0).T
        for i in range(16):
            blocks[8 * (2 * i + half) : 8 * (2 * i + half) + 8, :] = turned[8 * i : 8 * i + 8, :]
    for copy in copies:
        copy.wait()
    high = (maps[0] * H_SCALE + 0.5).astype(I32) - 32768
    low = (maps[1] * C_SCALE + 0.5).astype(I32)
    table[...] = (high << 16) | low
    to_scalar.wait()
    chunks = table.shape[0] // 8
    together = 8

    def first_chunk(block):
        return (bounds[8 * (block & 1), 8 * (block >> 1)] >> 25) + 64

    def last_chunk(block):
        return (bounds[23 + 8 * (block & 1), 8 * (block >> 1) + 7] >> 25) + 64

    def walk(index, carry):
        chunk, block = carry
        pending = []
        for _ in range(together):
            rows = pl.ds(pl.multiple_of(block * 8, 8), 8)
            key = blocks[rows, :]
            lane = (key >> 15) & (LANES - 1)
            line = (key >> 22) + 512
            value = jnp.zeros((8, LANES), I32)
            for offset in range(8):
                row = chunk * 8 + offset
                words = jnp.broadcast_to(table[pl.ds(row, 1), :], (8, LANES))
                taken = jnp.take_along_axis(words, lane, axis=1)
                value = jnp.where(line == row, taken, value)
            pending.append((rows, (line >> 3) == chunk, value))
            after = jnp.minimum(block + 1, REGISTERS - 1)
            stay = last_chunk(block) > chunk
            chunk = jnp.where(stay, chunk + 1, first_chunk(after))
            block = jnp.where(stay, block, after)
        for rows, mine, value in pending:
            found[rows, :] = jnp.where(mine, value, found[rows, :])
        return chunk, block

    lax.fori_loop(0, (REGISTERS + chunks) // together, walk, (first_chunk(0), jnp.int32(0)))
    highs, lows = [], []
    for register in range(REGISTERS):
        rows = slice(8 * register, 8 * register + 8)
        place = ((blocks[rows, :] & 32767) - 16384) << 16
        word = found[rows, :]
        highs.append(place | ((word >> 16) & 0xFFFF))
        lows.append(place | (word & 0xFFFF))
    steps = list(sort_steps(BY_LANE))
    for i in range(len(steps) + LAG):
        if i < len(steps):
            highs = advance(highs, steps[i])
        if i >= LAG:
            lows = advance(lows, steps[i - LAG])
    owners = wanted_ref.shape[1]
    blank = jnp.zeros((1, LANES), I32)
    for owner in range(2):
        out_ref[WIDTH * owner + 3 : WIDTH * owner + 4, :] = blank
        out_ref[WIDTH * (owners - 1 - owner) + 2 : WIDTH * (owners - 1 - owner) + 3, :] = blank
    for register in range(REGISTERS):
        slot, owner = register >> 4, 8 * (register & 15)
        word = (highs[register] << 16) | (lows[register] & 0xFFFF)
        out_ref[pl.ds(WIDTH * owner + slot, 8, stride=WIDTH), :] = word
        if slot == 0 and owner == 0:
            out_ref[pl.ds(2, 6, stride=WIDTH), :] = word[2:8]
        elif slot == 0:
            out_ref[pl.ds(WIDTH * (owner - 2) + 2, 8, stride=WIDTH), :] = word
        elif owner == owners - 8:
            out_ref[pl.ds(WIDTH * (owner + 2) + 3, 6, stride=WIDTH), :] = word[0:6]
        else:
            out_ref[pl.ds(WIDTH * (owner + 2) + 3, 8, stride=WIDTH), :] = word
    lane = lax.broadcasted_iota(I32, (1, LANES), 1)
    first, second = wanted_ref[0:1, :], wanted_ref[1:2, :]
    below = pltpu.roll(jnp.broadcast_to(first, (8, LANES)), LANES - 2, 1)[0:1]
    above = pltpu.roll(jnp.broadcast_to(second, (8, LANES)), 2, 1)[0:1]
    tiles = [
        jnp.where(first >= 0, first + DEEP, -1),
        jnp.where(second >= 0, second + DEEP, -1),
        jnp.where((below >= 0) & (below < DEEP) & (lane < owners - 2), below + (ROWS + DEEP), -1),
        jnp.where((above >= ROWS - DEEP) & (lane >= 2), above - (ROWS - DEEP), -1),
    ]
    turned = jnp.concatenate(tiles + [jnp.zeros((LANES - 4, LANES), I32)], axis=0).T
    for owner in range(0, owners, 8):
        out_ref[pl.ds(WIDTH * owner + WIDTH - 1, 8, stride=WIDTH), :] = turned[owner : owner + 8, :]


def sample(pixels, wanted, heights, confidence):
    flat = pltpu.VMEM(pixels.shape, I32)
    return pl.pallas_call(
        sample_kernel,
        out_shape=jax.ShapeDtypeStruct((WIDTH * wanted.shape[1], LANES), I32),
        in_specs=[
            pl.BlockSpec(memory_space=pltpu.VMEM),
            pl.BlockSpec(memory_space=pltpu.VMEM),
            pl.BlockSpec(memory_space=pl.ANY),
            pl.BlockSpec(memory_space=pl.ANY),
        ],
        out_specs=pl.BlockSpec(memory_space=pltpu.VMEM),
        scratch_shapes=[
            pltpu.VMEM((2,) + heights.shape, F32),
            pltpu.VMEM(heights.shape, I32),
            flat,
            flat,
            pltpu.VMEM((32, LANES), I32),
            pltpu.SMEM((32, LANES), I32),
            pltpu.SemaphoreType.DMA((3,)),
        ],
        compiler_params=pltpu.CompilerParams(vmem_limit_bytes=60 << 20),
        name="sample",
    )(pixels, wanted, heights, confidence)


def join_kernel(
    spot_ref, list_ref, words_ref, above_ref, below_ref, prior_hbm, weight_hbm,
    joined_ref, new_ref, edge_ref,
    order_ref, height, certainty, prior_ref, total, sems,
):
    inner = pl.ds(DEEP, ROWS)
    copies = [
        pltpu.make_async_copy(prior_hbm, prior_ref.at[inner], sems.at[0]),
        pltpu.make_async_copy(weight_hbm, total.at[inner], sems.at[1]),
    ]
    for copy in copies:
        copy.start()
    col = spot_ref[1]
    entries = words_ref.shape[0]
    word = words_ref[...]
    height[0:entries, :] = ((word >> 16) + 32768).astype(F32) * (0.5 / H_SCALE)
    certainty[0:entries, :] = (word & 0xFFFF).astype(F32) * (0.5 / C_SCALE)
    height[entries:, :] = jnp.zeros((8, LANES), F32)
    certainty[entries:, :] = jnp.zeros((8, LANES), F32)
    level = lax.broadcasted_iota(I32, (BINS, LANES), 0).astype(F32) * 0.5

    def pick(reader, count):
        for slot in range(WIDTH - 1):
            tile = list_ref[reader, slot]
            order_ref[count] = tile * 1024 + (WIDTH * reader + slot)
            count = count + jnp.where(tile >= 0, 1, 0)
        return count

    count = lax.fori_loop(0, list_ref.shape[0], pick, jnp.int32(0), unroll=4)
    for i in range(AT_ONCE):
        order_ref[count + i] = entries
    for copy in copies:
        copy.wait()
    for row in range(DEEP):
        prior_ref[row] = above_ref[row]
        prior_ref[ROWS + DEEP + row] = below_ref[row]
        total[row] = above_ref[DEEP + row]
        total[ROWS + DEEP + row] = below_ref[DEEP + row]
    joined_ref[...] = (2.0 * total[...]) * prior_ref[...]

    def term(place):
        code = order_ref[place]
        tile = code >> 10
        entry = code & 1023
        prior = prior_ref[tile]
        scaled = height[pl.ds(entry, 1), :] - level
        signed = jnp.clip(scaled, -2.0, 2.0)
        visible = jnp.clip(scaled + 4.0, 0.0, 2.0)
        mismatch = signed - (prior + prior)
        spread = 1.0 + mismatch * mismatch
        inverse = pl.reciprocal(spread, approx=True)
        inverse = inverse * (2.0 - spread * inverse)
        observed = (certainty[pl.ds(entry, 1), :] * visible) * inverse
        return tile, observed, observed * signed

    def step(index, carry):
        terms = [term(AT_ONCE * index + i) for i in range(AT_ONCE)]
        for tile, observed, weighted in terms:
            total[tile] += observed
            joined_ref[tile] += weighted
        return carry

    lax.fori_loop(0, (count + AT_ONCE - 1) // AT_ONCE, step, 0)
    lane = lax.broadcasted_iota(I32, (BINS, LANES), 1)
    source = jnp.where(col == 0, LANES - DEEP, 0)
    has_above = spot_ref[0] > 0
    has_below = spot_ref[0] < spot_ref[2]
    edge = jnp.zeros((BINS, LANES), F32)
    for row in range(EXT):
        value = (0.5 * joined_ref[row]) / total[row]
        if row < DEEP:
            value = jnp.where(has_above, value, 0.0)
        elif row >= ROWS + DEEP:
            value = jnp.where(has_below, value, 0.0)
        else:
            new_ref[row - DEEP] = total[row]
        joined_ref[row] = value
        start = row * DEEP
        moved = pltpu.roll(value, (start - source + LANES) % LANES, 1)
        edge = jnp.where((lane >= start) & (lane < start + DEEP), moved, edge)
    edge_ref[...] = edge


def join(spot, lists, words, above, below, prior, weight):
    rows, bins, lanes = prior.shape
    tall = (rows + 2 * DEEP, bins, lanes)
    vmem = pl.BlockSpec(memory_space=pltpu.VMEM)
    smem = pl.BlockSpec(memory_space=pltpu.SMEM)
    anywhere = pl.BlockSpec(memory_space=pl.ANY)
    column = pltpu.VMEM((words.shape[0] + 8, LANES), F32)
    return pl.pallas_call(
        join_kernel,
        out_shape=(
            jax.ShapeDtypeStruct(tall, F32),
            jax.ShapeDtypeStruct(prior.shape, F32),
            jax.ShapeDtypeStruct((BINS, LANES), F32),
        ),
        in_specs=[smem, smem, vmem, vmem, vmem, anywhere, anywhere],
        out_specs=(vmem, vmem, vmem),
        scratch_shapes=[
            pltpu.SMEM(((WIDTH - 1) * lists.shape[0] + AT_ONCE,), I32),
            column,
            column,
            pltpu.VMEM(tall, F32),
            pltpu.VMEM(tall, F32),
            pltpu.SemaphoreType.DMA((2,)),
        ],
        compiler_params=pltpu.CompilerParams(vmem_limit_bytes=JOIN_VMEM << 20),
        name="join",
    )(spot, lists, words, above, below, prior, weight)


def silu(value):
    half = 0.5 * value
    return half + half * jnp.tanh(half)


def weight_matrices(taps_ref, matrix):
    layers, bins, taps = taps_ref.shape
    tap = lax.broadcasted_iota(I32, (taps, 3 * BINS), 0)
    place = lax.broadcasted_iota(I32, (taps, 3 * BINS), 1)
    out_bin = lax.broadcasted_iota(I32, (BINS, 3 * BINS), 0)
    in_bin = lax.broadcasted_iota(I32, (BINS, 3 * BINS), 1) & (BINS - 1)
    same = (out_bin // GROUP) == (in_bin // GROUP)
    wanted = (place & (GROUP - 1)) * 9 + (place // BINS) * 3
    for offset in range(3):
        chosen = (tap == wanted + offset).astype(F32).astype(BF16)
        for layer in range(layers):
            spread = jnp.dot(taps_ref[layer], chosen, preferred_element_type=F32)
            matrix[layer, BINS * offset : BINS * (offset + 1), :] = jnp.where(same, spread, 0.0).astype(BF16)


def refine_kernel(
    spot_ref, taps_ref, joined_ref, side_ref, out_ref, matrix, current, active, side_active
):
    row_index, col, last_row = spot_ref[0], spot_ref[1], spot_ref[2]
    weight_matrices(taps_ref, matrix)
    lane = lax.broadcasted_iota(I32, (BINS, LANES), 1)
    has_above = row_index > 0
    has_below = row_index < last_row
    inside = ((lane >= DEEP * DEEP) | has_above) & ((lane < (ROWS + DEEP) * DEEP) | has_below)
    edge_lane = jnp.where(col == 0, LANES - 1, 0)
    at_edge = lane == edge_lane
    near = jnp.where(col == 0, 0, DEEP - 1)

    side_current = side_ref[...]
    side_active[...] = silu(side_current).astype(BF16)

    def fill(row, carry):
        active[0, row] = silu(joined_ref[row]).astype(BF16)
        return carry

    lax.fori_loop(0, EXT, fill, 0, unroll=EXT // 2)

    layers = taps_ref.shape[0]
    for layer in range(layers):
        now, later = layer % 2, (layer + 1) % 2
        taps = matrix[layer]
        inner = side_active[...].astype(F32)
        stack = jnp.concatenate(
            [pltpu.roll(inner, DEEP, 1), inner, pltpu.roll(inner, LANES - DEEP, 1)], axis=0
        ).astype(BF16)
        side_part = jnp.dot(taps, stack, preferred_element_type=F32)
        side_left, side_mid, side_right = (side_part[BINS * i : BINS * (i + 1)] for i in range(3))
        side_edge = jnp.where(col == 0, side_right, side_left)
        first = 1 + layer
        pairs = (EXT - 2 - 2 * layer) // 2
        final = layer == layers - 1

        def pair(step, injected):
            row = first + 2 * step
            planes = [active[now, row - 1 + i] for i in range(4)]
            stack = jnp.concatenate(
                [jnp.concatenate(planes[0:3], axis=0), jnp.concatenate(planes[1:4], axis=0)], axis=1
            )
            part = jnp.dot(taps, stack, preferred_element_type=F32)
            for i in range(2):
                here = row + i
                left, mid, right = (
                    part[BINS * k : BINS * (k + 1), LANES * i : LANES * (i + 1)] for k in range(3)
                )
                spot = here * DEEP + near
                moved = pltpu.roll(side_edge, (edge_lane - spot + LANES) % LANES, 1)
                response = mid + jnp.where(lane == 0, 0.0, pltpu.roll(left, 1, 1))
                response = response + jnp.where(lane == LANES - 1, 0.0, pltpu.roll(right, LANES - 1, 1))
                before = joined_ref[here] if layer == 0 else current[here]
                value = before + (response + jnp.where(at_edge, moved, 0.0))
                if final:
                    out_ref[here - DEEP] = value
                else:
                    current[here] = value
                    keep = ((here >= DEEP) | has_above) & ((here < ROWS + DEEP) | has_below)
                    active[later, here] = jnp.where(keep, silu(value), 0.0).astype(BF16)
                    outward = jnp.where(col == 0, left, right)
                    thrown = pltpu.roll(outward, (spot - edge_lane + LANES) % LANES, 1)
                    injected = jnp.where(lane == spot, thrown, injected)
            return injected

        def several(step, injected):
            for i in range(TOGETHER):
                injected = pair(TOGETHER * step + i, injected)
            return injected

        full = pairs // TOGETHER
        injected = lax.fori_loop(0, full, several, jnp.zeros((BINS, LANES), F32))
        for step in range(full * TOGETHER, pairs):
            injected = pair(step, injected)
        if not final:
            place = lane % DEEP
            from_left = jnp.where((place == 0) & (col == 0), injected, pltpu.roll(side_left, 1, 1))
            from_right = jnp.where((place == DEEP - 1) & (col != 0), injected, pltpu.roll(side_right, LANES - 1, 1))
            side_current = side_current + (side_mid + from_left + from_right)
            side_active[...] = jnp.where(inside, silu(side_current), 0.0).astype(BF16)


def refine(spot, taps, joined, side):
    vmem = pl.BlockSpec(memory_space=pltpu.VMEM)
    smem = pl.BlockSpec(memory_space=pltpu.SMEM)
    return pl.pallas_call(
        refine_kernel,
        out_shape=jax.ShapeDtypeStruct((ROWS,) + joined.shape[1:], F32),
        in_specs=[smem] + [vmem] * 3,
        out_specs=vmem,
        scratch_shapes=[
            pltpu.VMEM((taps.shape[0], 3 * BINS, 3 * BINS), BF16),
            pltpu.VMEM((EXT, BINS, LANES), F32),
            pltpu.VMEM((2, EXT, BINS, LANES), BF16),
            pltpu.VMEM((BINS, LANES), BF16),
        ],
        compiler_params=pltpu.CompilerParams(vmem_limit_bytes=16 << 20),
        name="refine",
    )(spot, taps, joined, side)


def on_device(tsdf_prior, prior_weight, depth_maps, confidence, frustum_tiles, pixel_index, conv_weights):
    row_count = lax.axis_size("row")
    spot = jnp.stack([lax.axis_index("row"), lax.axis_index("col"), jnp.int32(row_count - 1)]).astype(I32)
    readers = frustum_tiles.shape[1]
    both = ("row", "col")
    words = sample(
        pixel_index.reshape(-1, LANES),
        frustum_tiles[0].T,
        depth_maps.reshape(-1, LANES),
        confidence.reshape(-1, LANES),
    )
    width = WIDTH * LANES
    got = lax.all_to_all(words.reshape(readers, 1, width), both, split_axis=0, concat_axis=0, tiled=True)
    up = [(i, i + 1) for i in range(row_count - 1)]
    down = [(j, i) for i, j in up]
    above = lax.ppermute(jnp.concatenate([tsdf_prior[ROWS - DEEP :], prior_weight[ROWS - DEEP :]], axis=0), "row", up)
    below = lax.ppermute(jnp.concatenate([tsdf_prior[:DEEP], prior_weight[:DEEP]], axis=0), "row", down)
    start = (WIDTH - 1) * LANES
    joined, new_weight, edge = join(
        spot,
        got[:, 0, start : start + WIDTH - 1],
        got.reshape(WIDTH * readers, LANES),
        above,
        below,
        tsdf_prior,
        prior_weight,
    )
    side = lax.ppermute(edge, "col", [(0, 1), (1, 0)])
    layers = conv_weights.shape[0]
    refined = refine(spot, conv_weights.reshape(layers, BINS, GROUP * 9), joined, side)
    return refined, new_weight


def solution(mesh):
    placed = (
        P("row", None, "col"),
        P("row", None, "col"),
        P("row", None),
        P("row", None),
        P(("row", "col"), None, None),
        P(("row", "col"), None, None, None),
        P(),
    )
    return jax.shard_map(
        on_device,
        mesh=mesh,
        in_specs=placed,
        out_specs=(P("row", None, "col"), P("row", None, "col")),
        check_vma=False,
    )
```

```python
import jax
import jax.numpy as jnp
from jax import lax
from jax.experimental import pallas as pl
from jax.experimental.pallas import tpu as pltpu
from jax.sharding import PartitionSpec as P

LANES = 128
BINS = 64
ROWS = 32
DEEP = 3
EXT = ROWS + 2 * DEEP
GROUP = 16
AT_ONCE = 8
WIDTH = 5
JOIN_VMEM = 16
SENT = 4
H_SCALE = 1023.0
C_SCALE = 13000.0
F32 = jnp.float32
BF16 = jnp.bfloat16
I32 = jnp.int32


BY_BLOCK = [("v", 0), ("v", 1), ("v", 2), ("v", 3), ("s", 0), ("s", 1), ("s", 2), ("l", 0), ("l", 1), ("l", 2)]
BY_BLOCK += [("v", 4), ("l", 3), ("l", 4), ("l", 5), ("l", 6)]
BY_LANE = [("v", i) for i in range(5)] + [("s", i) for i in range(3)] + [("l", i) for i in range(7)]
REGISTERS = 32
LAG = 8


def along(kind):
    return lax.broadcasted_iota(I32, (8, LANES), 0 if kind == "s" else 1)


def exchange(parts, kind, bit):
    distance = 1 << bit
    if kind == "v":
        parts = list(parts)
        for low in range(REGISTERS):
            if low & distance == 0:
                one, two = parts[low], parts[low | distance]
                parts[low], parts[low | distance] = jnp.minimum(one, two), jnp.maximum(one, two)
        return parts
    axis = 0 if kind == "s" else 1
    size = (8, LANES)[axis]
    upper = (along(kind) & distance) != 0
    result = []
    for part in parts:
        from_low = pltpu.roll(part, distance, axis)
        from_high = from_low if 2 * distance == size else pltpu.roll(part, size - distance, axis)
        result.append(jnp.where(upper, jnp.maximum(part, from_low), jnp.minimum(part, from_high)))
    return result


def turn(parts, places):
    fixed = [bit for kind, bit in places if kind == "v"]
    mask = None
    for kind, bit in places:
        if kind != "v":
            one = -((along(kind) >> bit) & 1)
            mask = one if mask is None else mask ^ one
    result = []
    for register, part in enumerate(parts):
        if sum((register >> bit) & 1 for bit in fixed) % 2:
            part = ~part
        result.append(part if mask is None else part ^ mask)
    return result


def sort_steps(order):
    size = len(order)
    for phase in range(1, size + 1):
        yield "turn", [order[place] for place in (phase - 1, phase) if 0 < place < size and phase + place > 1]
        for place in range(phase - 1, -1, -1):
            yield "exchange", order[place]


def advance(parts, step):
    kind, what = step
    return turn(parts, what) if kind == "turn" else exchange(parts, *what)


def sample_kernel(pixel_ref, wanted_ref, height_hbm, conf_hbm, out_ref, maps, table, blocks, found, edges, bounds, sems):
    copies = [
        pltpu.make_async_copy(height_hbm, maps.at[0], sems.at[0]),
        pltpu.make_async_copy(conf_hbm, maps.at[1], sems.at[1]),
    ]
    for copy in copies:
        copy.start()
    parts = []
    for register in range(REGISTERS):
        pixel = pixel_ref[8 * register : 8 * register + 8, :]
        place = ((along("s") & 1) << 4) + (register >> 1)
        place = place + ((4 * (register & 1) + (along("s") >> 1)) << 5) + (along("l") << 8)
        parts.append(((pixel - 65536) << 15) | place)
    for step in sort_steps(BY_BLOCK):
        parts = advance(parts, step)
    for i, register in enumerate((0, 16, 15, 31)):
        edges[8 * i : 8 * i + 8, :] = parts[register]
    to_scalar = pltpu.make_async_copy(edges, bounds, sems.at[2])
    to_scalar.start()
    for half in range(2):
        turned = jnp.concatenate(parts[16 * half : 16 * half + 16], axis=0).T
        for i in range(16):
            blocks[8 * (2 * i + half) : 8 * (2 * i + half) + 8, :] = turned[8 * i : 8 * i + 8, :]
    for copy in copies:
        copy.wait()
    high = (maps[0] * H_SCALE + 0.5).astype(I32) - 32768
    low = (maps[1] * C_SCALE + 0.5).astype(I32)
    table[...] = (high << 16) | low
    to_scalar.wait()
    chunks = table.shape[0] // 8
    together = 8

    def first_chunk(block):
        return (bounds[8 * (block & 1), 8 * (block >> 1)] >> 25) + 64

    def last_chunk(block):
        return (bounds[23 + 8 * (block & 1), 8 * (block >> 1) + 7] >> 25) + 64

    def walk(index, carry):
        chunk, block = carry
        pending = []
        for _ in range(together):
            rows = pl.ds(pl.multiple_of(block * 8, 8), 8)
            key = blocks[rows, :]
            lane = (key >> 15) & (LANES - 1)
            line = (key >> 22) + 512
            value = jnp.zeros((8, LANES), I32)
            for offset in range(8):
                row = chunk * 8 + offset
                words = jnp.broadcast_to(table[pl.ds(row, 1), :], (8, LANES))
                taken = jnp.take_along_axis(words, lane, axis=1)
                value = jnp.where(line == row, taken, value)
            pending.append((rows, (line >> 3) == chunk, value))
            after = jnp.minimum(block + 1, REGISTERS - 1)
            stay = last_chunk(block) > chunk
            chunk = jnp.where(stay, chunk + 1, first_chunk(after))
            block = jnp.where(stay, block, after)
        for rows, mine, value in pending:
            found[rows, :] = jnp.where(mine, value, found[rows, :])
        return chunk, block

    lax.fori_loop(0, (REGISTERS + chunks) // together, walk, (first_chunk(0), jnp.int32(0)))
    highs, lows = [], []
    for register in range(REGISTERS):
        rows = slice(8 * register, 8 * register + 8)
        place = ((blocks[rows, :] & 32767) - 16384) << 16
        word = found[rows, :]
        highs.append(place | ((word >> 16) & 0xFFFF))
        lows.append(place | (word & 0xFFFF))
    steps = list(sort_steps(BY_LANE))
    for i in range(len(steps) + LAG):
        if i < len(steps):
            highs = advance(highs, steps[i])
        if i >= LAG:
            lows = advance(lows, steps[i - LAG])
    owners = wanted_ref.shape[1]
    blank = jnp.zeros((1, LANES), I32)
    for owner in range(2):
        out_ref[WIDTH * owner + 3 : WIDTH * owner + 4, :] = blank
        out_ref[WIDTH * (owners - 1 - owner) + 2 : WIDTH * (owners - 1 - owner) + 3, :] = blank
    for register in range(REGISTERS):
        slot, owner = register >> 4, 8 * (register & 15)
        word = (highs[register] << 16) | (lows[register] & 0xFFFF)
        out_ref[pl.ds(WIDTH * owner + slot, 8, stride=WIDTH), :] = word
        if slot == 0 and owner == 0:
            out_ref[pl.ds(2, 6, stride=WIDTH), :] = word[2:8]
        elif slot == 0:
            out_ref[pl.ds(WIDTH * (owner - 2) + 2, 8, stride=WIDTH), :] = word
        elif owner == owners - 8:
            out_ref[pl.ds(WIDTH * (owner + 2) + 3, 6, stride=WIDTH), :] = word[0:6]
        else:
            out_ref[pl.ds(WIDTH * (owner + 2) + 3, 8, stride=WIDTH), :] = word
    lane = lax.broadcasted_iota(I32, (1, LANES), 1)
    first, second = wanted_ref[0:1, :], wanted_ref[1:2, :]
    below = pltpu.roll(jnp.broadcast_to(first, (8, LANES)), LANES - 2, 1)[0:1]
    above = pltpu.roll(jnp.broadcast_to(second, (8, LANES)), 2, 1)[0:1]
    tiles = [
        jnp.where(first >= 0, first + DEEP, -1),
        jnp.where(second >= 0, second + DEEP, -1),
        jnp.where((below >= 0) & (below < DEEP) & (lane < owners - 2), below + (ROWS + DEEP), -1),
        jnp.where((above >= ROWS - DEEP) & (lane >= 2), above - (ROWS - DEEP), -1),
    ]
    turned = jnp.concatenate(tiles + [jnp.zeros((LANES - 4, LANES), I32)], axis=0).T
    for owner in range(0, owners, 8):
        out_ref[pl.ds(WIDTH * owner + WIDTH - 1, 8, stride=WIDTH), :] = turned[owner : owner + 8, :]


def sample(pixels, wanted, heights, confidence):
    flat = pltpu.VMEM(pixels.shape, I32)
    return pl.pallas_call(
        sample_kernel,
        out_shape=jax.ShapeDtypeStruct((WIDTH * wanted.shape[1], LANES), I32),
        in_specs=[
            pl.BlockSpec(memory_space=pltpu.VMEM),
            pl.BlockSpec(memory_space=pltpu.VMEM),
            pl.BlockSpec(memory_space=pl.ANY),
            pl.BlockSpec(memory_space=pl.ANY),
        ],
        out_specs=pl.BlockSpec(memory_space=pltpu.VMEM),
        scratch_shapes=[
            pltpu.VMEM((2,) + heights.shape, F32),
            pltpu.VMEM(heights.shape, I32),
            flat,
            flat,
            pltpu.VMEM((32, LANES), I32),
            pltpu.SMEM((32, LANES), I32),
            pltpu.SemaphoreType.DMA((3,)),
        ],
        compiler_params=pltpu.CompilerParams(vmem_limit_bytes=60 << 20),
        name="sample",
    )(pixels, wanted, heights, confidence)


def join_kernel(
    spot_ref, list_ref, words_ref, above_ref, below_ref, prior_hbm, weight_hbm,
    joined_ref, new_hbm, edge_ref,
    order_ref, height, certainty, prior_ref, total, sems,
):
    inner = pl.ds(DEEP, ROWS)
    copies = [
        pltpu.make_async_copy(prior_hbm, prior_ref.at[inner], sems.at[0]),
        pltpu.make_async_copy(weight_hbm, total.at[inner], sems.at[1]),
    ]
    for copy in copies:
        copy.start()
    col = spot_ref[1]
    entries = words_ref.shape[0]
    word = words_ref[...]
    height[0:entries, :] = ((word >> 16) + 32768).astype(F32) * (0.5 / H_SCALE)
    certainty[0:entries, :] = (word & 0xFFFF).astype(F32) * (0.5 / C_SCALE)
    height[entries:, :] = jnp.zeros((8, LANES), F32)
    certainty[entries:, :] = jnp.zeros((8, LANES), F32)
    level = lax.broadcasted_iota(I32, (BINS, LANES), 0).astype(F32) * 0.5

    half = list_ref.shape[0] // 2
    room = order_ref.shape[0] // 2

    def pick(step, counts):
        counts = list(counts)
        for slot in range(WIDTH - 1):
            for side in range(2):
                reader = step + half * side
                tile = list_ref[reader, slot]
                order_ref[room * side + counts[side]] = tile * 1024 + (WIDTH * reader + slot)
                counts[side] = counts[side] + jnp.where(tile >= 0, 1, 0)
        return tuple(counts)

    counts = lax.fori_loop(0, half, pick, (jnp.int32(0), jnp.int32(0)), unroll=4)
    for side in range(2):
        for i in range(AT_ONCE):
            order_ref[room * side + counts[side] + i] = entries
    for copy in copies:
        copy.wait()
    for row in range(DEEP):
        prior_ref[row] = above_ref[row]
        prior_ref[ROWS + DEEP + row] = below_ref[row]
        total[row] = above_ref[DEEP + row]
        total[ROWS + DEEP + row] = below_ref[DEEP + row]
    joined_ref[...] = (2.0 * total[...]) * prior_ref[...]

    def term(place):
        code = order_ref[place]
        tile = code >> 10
        entry = code & 1023
        prior = prior_ref[tile]
        scaled = height[pl.ds(entry, 1), :] - level
        signed = jnp.clip(scaled, -2.0, 2.0)
        visible = jnp.clip(scaled + 4.0, 0.0, 2.0)
        mismatch = signed - (prior + prior)
        spread = 1.0 + mismatch * mismatch
        inverse = pl.reciprocal(spread, approx=True)
        inverse = inverse * (2.0 - spread * inverse)
        observed = (certainty[pl.ds(entry, 1), :] * visible) * inverse
        return tile, observed, observed * signed

    def step(index, carry):
        terms = [term(AT_ONCE * index + i) for i in range(AT_ONCE)]
        for tile, observed, weighted in terms:
            total[tile] += observed
            joined_ref[tile] += weighted
        return carry

    steps = [(count + AT_ONCE - 1) // AT_ONCE for count in counts]

    def either(index, carry):
        return step(jnp.where(index < steps[0], index, index - steps[0] + room // AT_ONCE), carry)

    lax.fori_loop(0, steps[0] + steps[1], either, 0)
    leaving = pltpu.make_async_copy(total.at[inner], new_hbm, sems.at[0])
    leaving.start()
    lane = lax.broadcasted_iota(I32, (BINS, LANES), 1)
    source = jnp.where(col == 0, LANES - DEEP, 0)
    has_above = spot_ref[0] > 0
    has_below = spot_ref[0] < spot_ref[2]
    edge = jnp.zeros((BINS, LANES), F32)
    for row in range(EXT):
        inverse = pl.reciprocal(total[row], approx=True)
        value = (0.5 * joined_ref[row]) * (inverse * (2.0 - total[row] * inverse))
        if row < DEEP:
            value = jnp.where(has_above, value, 0.0)
        elif row >= ROWS + DEEP:
            value = jnp.where(has_below, value, 0.0)
        joined_ref[row] = value
        start = row * DEEP
        moved = pltpu.roll(value, (start - source + LANES) % LANES, 1)
        edge = jnp.where((lane >= start) & (lane < start + DEEP), moved, edge)
    edge_ref[...] = edge
    leaving.wait()


def join(spot, lists, words, above, below, prior, weight):
    rows, bins, lanes = prior.shape
    tall = (rows + 2 * DEEP, bins, lanes)
    vmem = pl.BlockSpec(memory_space=pltpu.VMEM)
    smem = pl.BlockSpec(memory_space=pltpu.SMEM)
    anywhere = pl.BlockSpec(memory_space=pl.ANY)
    column = pltpu.VMEM((words.shape[0] + 8, LANES), F32)
    return pl.pallas_call(
        join_kernel,
        out_shape=(
            jax.ShapeDtypeStruct(tall, F32),
            jax.ShapeDtypeStruct(prior.shape, F32),
            jax.ShapeDtypeStruct((BINS, LANES), F32),
        ),
        in_specs=[smem, smem, vmem, vmem, vmem, anywhere, anywhere],
        out_specs=(vmem, anywhere, vmem),
        scratch_shapes=[
            pltpu.SMEM(((WIDTH - 1) * lists.shape[0] + 2 * AT_ONCE,), I32),
            column,
            column,
            pltpu.VMEM(tall, F32),
            pltpu.VMEM(tall, F32),
            pltpu.SemaphoreType.DMA((2,)),
        ],
        compiler_params=pltpu.CompilerParams(vmem_limit_bytes=JOIN_VMEM << 20),
        name="join",
    )(spot, lists, words, above, below, prior, weight)


def silu(value):
    half = 0.5 * value
    return half + half * jnp.tanh(half)


def weight_kernel(taps_ref, matrix):
    layers, bins, taps = taps_ref.shape
    tap = lax.broadcasted_iota(I32, (taps, 3 * BINS), 0)
    place = lax.broadcasted_iota(I32, (taps, 3 * BINS), 1)
    out_bin = lax.broadcasted_iota(I32, (BINS, 3 * BINS), 0)
    in_bin = lax.broadcasted_iota(I32, (BINS, 3 * BINS), 1) & (BINS - 1)
    same = (out_bin // GROUP) == (in_bin // GROUP)
    wanted = (place & (GROUP - 1)) * 9 + (place // BINS) * 3
    for offset in range(3):
        chosen = (tap == wanted + offset).astype(F32).astype(BF16)
        for layer in range(layers):
            spread = jnp.dot(taps_ref[layer], chosen, preferred_element_type=F32)
            matrix[layer, BINS * offset : BINS * (offset + 1), :] = jnp.where(same, spread, 0.0).astype(BF16)


def tap_matrices(taps):
    return pl.pallas_call(
        weight_kernel,
        out_shape=jax.ShapeDtypeStruct((taps.shape[0], 3 * BINS, 3 * BINS), BF16),
        in_specs=[pl.BlockSpec(memory_space=pltpu.VMEM)],
        out_specs=pl.BlockSpec(memory_space=pltpu.VMEM),
        compiler_params=pltpu.CompilerParams(vmem_limit_bytes=16 << 20),
        name="tap_matrices",
    )(taps)


def refine_kernel(
    spot_ref, matrix, joined_ref, side_ref, out_hbm, out_ref, current, active, side_active, sems
):
    row_index, col, last_row = spot_ref[0], spot_ref[1], spot_ref[2]
    lane = lax.broadcasted_iota(I32, (BINS, LANES), 1)
    has_above = row_index > 0
    has_below = row_index < last_row
    leaving = []
    inside = ((lane >= DEEP * DEEP) | has_above) & ((lane < (ROWS + DEEP) * DEEP) | has_below)
    edge_lane = jnp.where(col == 0, LANES - 1, 0)
    at_edge = lane == edge_lane
    near = jnp.where(col == 0, 0, DEEP - 1)

    side_current = side_ref[...]
    side_active[...] = silu(side_current).astype(BF16)

    def fill(row, carry):
        active[0, row] = silu(joined_ref[row]).astype(BF16)
        return carry

    lax.fori_loop(0, EXT, fill, 0, unroll=EXT)

    layers = matrix.shape[0]
    for layer in range(layers):
        now, later = layer % 2, (layer + 1) % 2
        taps = matrix[layer]
        inner = side_active[...].astype(F32)
        stack = jnp.concatenate(
            [pltpu.roll(inner, DEEP, 1), inner, pltpu.roll(inner, LANES - DEEP, 1)], axis=0
        ).astype(BF16)
        side_part = jnp.dot(taps, stack, preferred_element_type=F32)
        side_left, side_mid, side_right = (side_part[BINS * i : BINS * (i + 1)] for i in range(3))
        side_edge = jnp.where(col == 0, side_right, side_left)
        first = 1 + layer
        pairs = (EXT - 2 - 2 * layer) // 2
        final = layer == layers - 1

        def pair(step, injected):
            row = first + 2 * step
            planes = [active[now, row - 1 + i] for i in range(4)]
            stack = jnp.concatenate(
                [jnp.concatenate(planes[0:3], axis=0), jnp.concatenate(planes[1:4], axis=0)], axis=1
            )
            part = jnp.dot(taps, stack, preferred_element_type=F32)
            for i in range(2):
                here = row + i
                left, mid, right = (
                    part[BINS * k : BINS * (k + 1), LANES * i : LANES * (i + 1)] for k in range(3)
                )
                spot = here * DEEP + near
                moved = pltpu.roll(side_edge, (edge_lane - spot + LANES) % LANES, 1)
                response = mid + jnp.where(lane == 0, 0.0, pltpu.roll(left, 1, 1))
                response = response + jnp.where(lane == LANES - 1, 0.0, pltpu.roll(right, LANES - 1, 1))
                before = joined_ref[here] if layer == 0 else current[here]
                value = before + (response + jnp.where(at_edge, moved, 0.0))
                if final:
                    out_ref[here - DEEP] = value
                else:
                    current[here] = value
                    keep = ((here >= DEEP) | has_above) & ((here < ROWS + DEEP) | has_below)
                    active[later, here] = jnp.where(keep, silu(value), 0.0).astype(BF16)
                    outward = jnp.where(col == 0, left, right)
                    thrown = pltpu.roll(outward, (spot - edge_lane + LANES) % LANES, 1)
                    injected = jnp.where(lane == spot, thrown, injected)
            return injected

        injected = jnp.zeros((BINS, LANES), F32)
        for step in range(pairs):
            injected = pair(step, injected)
            if final and (step + 1) % SENT == 0:
                rows = pl.ds(2 * (step + 1 - SENT), 2 * SENT)
                copy = pltpu.make_async_copy(out_ref.at[rows], out_hbm.at[rows], sems.at[len(leaving)])
                copy.start()
                leaving.append(copy)
        if not final:
            place = lane % DEEP
            from_left = jnp.where((place == 0) & (col == 0), injected, pltpu.roll(side_left, 1, 1))
            from_right = jnp.where((place == DEEP - 1) & (col != 0), injected, pltpu.roll(side_right, LANES - 1, 1))
            side_current = side_current + (side_mid + from_left + from_right)
            side_active[...] = jnp.where(inside, silu(side_current), 0.0).astype(BF16)
    for copy in leaving:
        copy.wait()


def refine(spot, matrix, joined, side):
    vmem = pl.BlockSpec(memory_space=pltpu.VMEM)
    smem = pl.BlockSpec(memory_space=pltpu.SMEM)
    anywhere = pl.BlockSpec(memory_space=pl.ANY)
    flat = (ROWS,) + joined.shape[1:]
    return pl.pallas_call(
        refine_kernel,
        out_shape=jax.ShapeDtypeStruct(flat, F32),
        in_specs=[smem, vmem, vmem, vmem],
        out_specs=anywhere,
        scratch_shapes=[
            pltpu.VMEM(flat, F32),
            pltpu.VMEM(joined.shape, F32),
            pltpu.VMEM((2,) + joined.shape, BF16),
            pltpu.VMEM((BINS, LANES), BF16),
            pltpu.SemaphoreType.DMA((ROWS // (2 * SENT),)),
        ],
        compiler_params=pltpu.CompilerParams(vmem_limit_bytes=16 << 20),
        name="refine",
    )(spot, matrix, joined, side)


def on_device(tsdf_prior, prior_weight, depth_maps, confidence, frustum_tiles, pixel_index, conv_weights):
    row_count = lax.axis_size("row")
    spot = jnp.stack([lax.axis_index("row"), lax.axis_index("col"), jnp.int32(row_count - 1)]).astype(I32)
    readers = frustum_tiles.shape[1]
    both = ("row", "col")
    words = sample(
        pixel_index.reshape(-1, LANES),
        frustum_tiles[0].T,
        depth_maps.reshape(-1, LANES),
        confidence.reshape(-1, LANES),
    )
    width = WIDTH * LANES
    got = lax.all_to_all(words.reshape(readers, 1, width), both, split_axis=0, concat_axis=0, tiled=True)
    up = [(i, i + 1) for i in range(row_count - 1)]
    down = [(j, i) for i, j in up]
    above = lax.ppermute(jnp.concatenate([tsdf_prior[ROWS - DEEP :], prior_weight[ROWS - DEEP :]], axis=0), "row", up)
    below = lax.ppermute(jnp.concatenate([tsdf_prior[:DEEP], prior_weight[:DEEP]], axis=0), "row", down)
    layers = conv_weights.shape[0]
    matrix = tap_matrices(conv_weights.reshape(layers, BINS, GROUP * 9))
    above, matrix = lax.optimization_barrier((above, matrix))
    start = (WIDTH - 1) * LANES
    joined, new_weight, edge = join(
        spot,
        got[:, 0, start : start + WIDTH - 1],
        got.reshape(WIDTH * readers, LANES),
        above,
        below,
        tsdf_prior,
        prior_weight,
    )
    side = lax.ppermute(edge, "col", [(0, 1), (1, 0)])
    refined = refine(spot, matrix, joined, side)
    return refined, new_weight


def solution(mesh):
    placed = (
        P("row", None, "col"),
        P("row", None, "col"),
        P("row", None),
        P("row", None),
        P(("row", "col"), None, None),
        P(("row", "col"), None, None, None),
        P(),
    )
    return jax.shard_map(
        on_device,
        mesh=mesh,
        in_specs=placed,
        out_specs=(P("row", None, "col"), P("row", None, "col")),
        check_vma=False,
    )
```

```python
import jax
import jax.numpy as jnp
from jax import lax
from jax.experimental import pallas as pl
from jax.experimental.pallas import tpu as pltpu
from jax.sharding import PartitionSpec as P

LANES = 128
BINS = 64
ROWS = 32
DEEP = 3
EXT = ROWS + 2 * DEEP
GROUP = 16
AT_ONCE = 4
WIDTH = 5
JOIN_VMEM = 16
SENT = 4
H_SCALE = 1023.0
C_SCALE = 13000.0
F32 = jnp.float32
BF16 = jnp.bfloat16
I32 = jnp.int32


BY_BLOCK = [("v", 0), ("v", 1), ("v", 2), ("v", 3), ("s", 0), ("s", 1), ("s", 2), ("l", 0), ("l", 1), ("l", 2)]
BY_BLOCK += [("v", 4), ("l", 3), ("l", 4), ("l", 5), ("l", 6)]
BY_LANE = [("v", i) for i in range(5)] + [("s", i) for i in range(3)] + [("l", i) for i in range(7)]
REGISTERS = 32
LAG = 8


def along(kind):
    return lax.broadcasted_iota(I32, (8, LANES), 0 if kind == "s" else 1)


def exchange(parts, kind, bit):
    distance = 1 << bit
    if kind == "v":
        parts = list(parts)
        for low in range(REGISTERS):
            if low & distance == 0:
                one, two = parts[low], parts[low | distance]
                parts[low], parts[low | distance] = jnp.minimum(one, two), jnp.maximum(one, two)
        return parts
    axis = 0 if kind == "s" else 1
    size = (8, LANES)[axis]
    upper = (along(kind) & distance) != 0
    result = []
    for part in parts:
        from_low = pltpu.roll(part, distance, axis)
        from_high = from_low if 2 * distance == size else pltpu.roll(part, size - distance, axis)
        result.append(jnp.where(upper, jnp.maximum(part, from_low), jnp.minimum(part, from_high)))
    return result


def turn(parts, places):
    fixed = [bit for kind, bit in places if kind == "v"]
    mask = None
    for kind, bit in places:
        if kind != "v":
            one = -((along(kind) >> bit) & 1)
            mask = one if mask is None else mask ^ one
    result = []
    for register, part in enumerate(parts):
        if sum((register >> bit) & 1 for bit in fixed) % 2:
            part = ~part
        result.append(part if mask is None else part ^ mask)
    return result


def sort_steps(order):
    size = len(order)
    for phase in range(1, size + 1):
        yield "turn", [order[place] for place in (phase - 1, phase) if 0 < place < size and phase + place > 1]
        for place in range(phase - 1, -1, -1):
            yield "exchange", order[place]


def advance(parts, step):
    kind, what = step
    return turn(parts, what) if kind == "turn" else exchange(parts, *what)


def sample_kernel(pixel_ref, wanted_ref, height_hbm, conf_hbm, out_ref, maps, table, blocks, found, edges, bounds, sems):
    copies = [
        pltpu.make_async_copy(height_hbm, maps.at[0], sems.at[0]),
        pltpu.make_async_copy(conf_hbm, maps.at[1], sems.at[1]),
    ]
    for copy in copies:
        copy.start()
    parts = []
    for register in range(REGISTERS):
        pixel = pixel_ref[8 * register : 8 * register + 8, :]
        place = ((along("s") & 1) << 4) + (register >> 1)
        place = place + ((4 * (register & 1) + (along("s") >> 1)) << 5) + (along("l") << 8)
        parts.append(((pixel - 65536) << 15) | place)
    for step in sort_steps(BY_BLOCK):
        parts = advance(parts, step)
    for i, register in enumerate((0, 16, 15, 31)):
        edges[8 * i : 8 * i + 8, :] = parts[register]
    to_scalar = pltpu.make_async_copy(edges, bounds, sems.at[2])
    to_scalar.start()
    for half in range(2):
        turned = jnp.concatenate(parts[16 * half : 16 * half + 16], axis=0).T
        for i in range(16):
            blocks[8 * (2 * i + half) : 8 * (2 * i + half) + 8, :] = turned[8 * i : 8 * i + 8, :]
    for copy in copies:
        copy.wait()
    high = (maps[0] * H_SCALE + 0.5).astype(I32) - 32768
    low = (maps[1] * C_SCALE + 0.5).astype(I32)
    table[...] = (high << 16) | low
    to_scalar.wait()
    chunks = table.shape[0] // 8
    together = 16

    def first_chunk(block):
        return (bounds[8 * (block & 1), 8 * (block >> 1)] >> 25) + 64

    def last_chunk(block):
        return (bounds[23 + 8 * (block & 1), 8 * (block >> 1) + 7] >> 25) + 64

    def walk(index, carry):
        chunk, block = carry
        pending = []
        for _ in range(together):
            rows = pl.ds(pl.multiple_of(block * 8, 8), 8)
            key = blocks[rows, :]
            lane = (key >> 15) & (LANES - 1)
            line = (key >> 22) + 512
            value = jnp.zeros((8, LANES), I32)
            for offset in range(8):
                row = chunk * 8 + offset
                words = jnp.broadcast_to(table[pl.ds(row, 1), :], (8, LANES))
                taken = jnp.take_along_axis(words, lane, axis=1)
                value = jnp.where(line == row, taken, value)
            pending.append((rows, (line >> 3) == chunk, value))
            after = jnp.minimum(block + 1, REGISTERS - 1)
            stay = last_chunk(block) > chunk
            chunk = jnp.where(stay, chunk + 1, first_chunk(after))
            block = jnp.where(stay, block, after)
        for rows, mine, value in pending:
            found[rows, :] = jnp.where(mine, value, found[rows, :])
        return chunk, block

    lax.fori_loop(0, (REGISTERS + chunks) // together, walk, (first_chunk(0), jnp.int32(0)))
    highs, lows = [], []
    for register in range(REGISTERS):
        rows = slice(8 * register, 8 * register + 8)
        place = ((blocks[rows, :] & 32767) - 16384) << 16
        word = found[rows, :]
        highs.append(place | ((word >> 16) & 0xFFFF))
        lows.append(place | (word & 0xFFFF))
    steps = list(sort_steps(BY_LANE))
    for i in range(len(steps) + LAG):
        if i < len(steps):
            highs = advance(highs, steps[i])
        if i >= LAG:
            lows = advance(lows, steps[i - LAG])
    owners = wanted_ref.shape[1]
    blank = jnp.zeros((1, LANES), I32)
    for owner in range(2):
        out_ref[WIDTH * owner + 3 : WIDTH * owner + 4, :] = blank
        out_ref[WIDTH * (owners - 1 - owner) + 2 : WIDTH * (owners - 1 - owner) + 3, :] = blank
    for register in range(REGISTERS):
        slot, owner = register >> 4, 8 * (register & 15)
        word = (highs[register] << 16) | (lows[register] & 0xFFFF)
        out_ref[pl.ds(WIDTH * owner + slot, 8, stride=WIDTH), :] = word
        if slot == 0 and owner == 0:
            out_ref[pl.ds(2, 6, stride=WIDTH), :] = word[2:8]
        elif slot == 0:
            out_ref[pl.ds(WIDTH * (owner - 2) + 2, 8, stride=WIDTH), :] = word
        elif owner == owners - 8:
            out_ref[pl.ds(WIDTH * (owner + 2) + 3, 6, stride=WIDTH), :] = word[0:6]
        else:
            out_ref[pl.ds(WIDTH * (owner + 2) + 3, 8, stride=WIDTH), :] = word
    lane = lax.broadcasted_iota(I32, (1, LANES), 1)
    first, second = wanted_ref[0:1, :], wanted_ref[1:2, :]
    below = pltpu.roll(jnp.broadcast_to(first, (8, LANES)), LANES - 2, 1)[0:1]
    above = pltpu.roll(jnp.broadcast_to(second, (8, LANES)), 2, 1)[0:1]
    tiles = [
        jnp.where(first >= 0, first + DEEP, -1),
        jnp.where(second >= 0, second + DEEP, -1),
        jnp.where((below >= 0) & (below < DEEP) & (lane < owners - 2), below + (ROWS + DEEP), -1),
        jnp.where((above >= ROWS - DEEP) & (lane >= 2), above - (ROWS - DEEP), -1),
    ]
    turned = jnp.concatenate(tiles + [jnp.zeros((LANES - 4, LANES), I32)], axis=0).T
    for owner in range(0, owners, 8):
        out_ref[pl.ds(WIDTH * owner + WIDTH - 1, 8, stride=WIDTH), :] = turned[owner : owner + 8, :]


def sample(pixels, wanted, heights, confidence):
    flat = pltpu.VMEM(pixels.shape, I32)
    return pl.pallas_call(
        sample_kernel,
        out_shape=jax.ShapeDtypeStruct((WIDTH * wanted.shape[1], LANES), I32),
        in_specs=[
            pl.BlockSpec(memory_space=pltpu.VMEM),
            pl.BlockSpec(memory_space=pltpu.VMEM),
            pl.BlockSpec(memory_space=pl.ANY),
            pl.BlockSpec(memory_space=pl.ANY),
        ],
        out_specs=pl.BlockSpec(memory_space=pltpu.VMEM),
        scratch_shapes=[
            pltpu.VMEM((2,) + heights.shape, F32),
            pltpu.VMEM(heights.shape, I32),
            flat,
            flat,
            pltpu.VMEM((32, LANES), I32),
            pltpu.SMEM((32, LANES), I32),
            pltpu.SemaphoreType.DMA((3,)),
        ],
        compiler_params=pltpu.CompilerParams(vmem_limit_bytes=60 << 20),
        name="sample",
    )(pixels, wanted, heights, confidence)


def join_kernel(
    spot_ref, list_ref, words_ref, above_ref, below_ref, prior_hbm, weight_hbm,
    joined_ref, new_hbm, edge_ref,
    order_ref, height, certainty, prior_ref, total, sems,
):
    inner = pl.ds(DEEP, ROWS)
    copies = [
        pltpu.make_async_copy(prior_hbm, prior_ref.at[inner], sems.at[0]),
        pltpu.make_async_copy(weight_hbm, total.at[inner], sems.at[1]),
    ]
    for copy in copies:
        copy.start()
    col = spot_ref[1]
    entries = words_ref.shape[0]
    word = words_ref[...]
    height[0:entries, :] = ((word >> 16) + 32768).astype(F32) * (0.5 / H_SCALE)
    certainty[0:entries, :] = (word & 0xFFFF).astype(F32) * (0.5 / C_SCALE)
    height[entries:, :] = jnp.zeros((8, LANES), F32)
    certainty[entries:, :] = jnp.zeros((8, LANES), F32)
    level = lax.broadcasted_iota(I32, (BINS, LANES), 0).astype(F32) * 0.5

    half = list_ref.shape[0] // 2
    room = order_ref.shape[0] // 2

    def pick(step, counts):
        counts = list(counts)
        codes = [[list_ref[2 * step + i + half * side, slot] for i in range(2) for slot in range(WIDTH - 1)] for side in range(2)]
        for pair in zip(*codes):
            for side in range(2):
                order_ref[room * side + counts[side]] = pair[side]
                counts[side] = counts[side] + (1 + (pair[side] >> 31))
        return tuple(counts)

    counts = lax.fori_loop(0, half // 2, pick, (jnp.int32(0), jnp.int32(0)), unroll=2)
    for side in range(2):
        for i in range(AT_ONCE):
            order_ref[room * side + counts[side] + i] = entries
    for copy in copies:
        copy.wait()
    for row in range(DEEP):
        prior_ref[row] = above_ref[row].astype(F32)
        prior_ref[ROWS + DEEP + row] = below_ref[row].astype(F32)
        total[row] = above_ref[DEEP + row].astype(F32)
        total[ROWS + DEEP + row] = below_ref[DEEP + row].astype(F32)
    for row in range(EXT):
        twice = 2.0 * prior_ref[row]
        prior_ref[row] = twice
        joined_ref[row] = total[row] * twice

    def term(place):
        code = order_ref[place]
        tile = code >> 10
        entry = code & 1023
        twice = prior_ref[tile]
        scaled = height[pl.ds(entry, 1), :] - level
        signed = jnp.clip(scaled, -2.0, 2.0)
        visible = jnp.clip(scaled + 4.0, 0.0, 2.0)
        mismatch = signed - twice
        spread = 1.0 + mismatch * mismatch
        inverse = pl.reciprocal(spread, approx=True)
        observed = (certainty[pl.ds(entry, 1), :] * visible) * inverse
        return tile, observed, observed * signed

    def step(index, carry):
        terms = [term(AT_ONCE * index + i) for i in range(AT_ONCE)]
        for tile, observed, weighted in terms:
            total[tile] += observed
            joined_ref[tile] += weighted
        return carry

    steps = [(count + AT_ONCE - 1) // AT_ONCE for count in counts]

    def either(index, carry):
        return step(jnp.where(index < steps[0], index, index - steps[0] + room // AT_ONCE), carry)

    lax.fori_loop(0, steps[0] + steps[1], either, 0)
    leaving = pltpu.make_async_copy(total.at[inner], new_hbm, sems.at[0])
    leaving.start()
    lane = lax.broadcasted_iota(I32, (BINS, LANES), 1)
    source = jnp.where(col == 0, LANES - DEEP, 0)
    has_above = spot_ref[0] > 0
    has_below = spot_ref[0] < spot_ref[2]
    edge = jnp.zeros((BINS, LANES), F32)
    for row in range(EXT):
        inverse = pl.reciprocal(total[row], approx=True)
        value = (0.5 * joined_ref[row]) * inverse
        if row < DEEP:
            value = jnp.where(has_above, value, 0.0)
        elif row >= ROWS + DEEP:
            value = jnp.where(has_below, value, 0.0)
        joined_ref[row] = value
        start = row * DEEP
        moved = pltpu.roll(value, (start - source + LANES) % LANES, 1)
        edge = jnp.where((lane >= start) & (lane < start + DEEP), moved, edge)
    edge_ref[...] = edge
    leaving.wait()


def join(spot, lists, words, above, below, prior, weight):
    rows, bins, lanes = prior.shape
    tall = (rows + 2 * DEEP, bins, lanes)
    vmem = pl.BlockSpec(memory_space=pltpu.VMEM)
    smem = pl.BlockSpec(memory_space=pltpu.SMEM)
    anywhere = pl.BlockSpec(memory_space=pl.ANY)
    column = pltpu.VMEM((words.shape[0] + 8, LANES), F32)
    return pl.pallas_call(
        join_kernel,
        out_shape=(
            jax.ShapeDtypeStruct(tall, F32),
            jax.ShapeDtypeStruct(prior.shape, F32),
            jax.ShapeDtypeStruct((BINS, LANES), F32),
        ),
        in_specs=[smem, smem, vmem, vmem, vmem, anywhere, anywhere],
        out_specs=(vmem, anywhere, vmem),
        scratch_shapes=[
            pltpu.SMEM(((WIDTH - 1) * lists.shape[0] + 2 * AT_ONCE,), I32),
            column,
            column,
            pltpu.VMEM(tall, F32),
            pltpu.VMEM(tall, F32),
            pltpu.SemaphoreType.DMA((2,)),
        ],
        compiler_params=pltpu.CompilerParams(vmem_limit_bytes=JOIN_VMEM << 20),
        name="join",
    )(spot, lists, words, above, below, prior, weight)


def silu(value):
    half = 0.5 * value
    return half + half * jnp.tanh(half)


def weight_kernel(taps_ref, matrix):
    layers, bins, taps = taps_ref.shape
    tap = lax.broadcasted_iota(I32, (taps, 3 * BINS), 0)
    place = lax.broadcasted_iota(I32, (taps, 3 * BINS), 1)
    out_bin = lax.broadcasted_iota(I32, (BINS, 3 * BINS), 0)
    in_bin = lax.broadcasted_iota(I32, (BINS, 3 * BINS), 1) & (BINS - 1)
    same = (out_bin // GROUP) == (in_bin // GROUP)
    wanted = (place & (GROUP - 1)) * 9 + (place // BINS) * 3
    for offset in range(3):
        chosen = (tap == wanted + offset).astype(F32).astype(BF16)
        for layer in range(layers):
            spread = jnp.dot(taps_ref[layer], chosen, preferred_element_type=F32)
            matrix[layer, BINS * offset : BINS * (offset + 1), :] = jnp.where(same, spread, 0.0).astype(BF16)


def tap_matrices(taps):
    return pl.pallas_call(
        weight_kernel,
        out_shape=jax.ShapeDtypeStruct((taps.shape[0], 3 * BINS, 3 * BINS), BF16),
        in_specs=[pl.BlockSpec(memory_space=pltpu.VMEM)],
        out_specs=pl.BlockSpec(memory_space=pltpu.VMEM),
        compiler_params=pltpu.CompilerParams(vmem_limit_bytes=16 << 20),
        name="tap_matrices",
    )(taps)


def refine_kernel(
    spot_ref, matrix, joined_ref, side_ref, out_hbm, out_ref, current, active, side_active, sems
):
    row_index, col, last_row = spot_ref[0], spot_ref[1], spot_ref[2]
    lane = lax.broadcasted_iota(I32, (BINS, LANES), 1)
    has_above = row_index > 0
    has_below = row_index < last_row
    leaving = []
    inside = ((lane >= DEEP * DEEP) | has_above) & ((lane < (ROWS + DEEP) * DEEP) | has_below)
    edge_lane = jnp.where(col == 0, LANES - 1, 0)
    at_edge = lane == edge_lane
    near = jnp.where(col == 0, 0, DEEP - 1)

    side_current = side_ref[...]
    side_active[...] = silu(side_current).astype(BF16)

    def fill(row, carry):
        active[0, row] = silu(joined_ref[row]).astype(BF16)
        return carry

    lax.fori_loop(0, EXT, fill, 0, unroll=EXT)

    layers = matrix.shape[0]
    for layer in range(layers):
        now, later = layer % 2, (layer + 1) % 2
        taps = matrix[layer]
        inner = side_active[...].astype(F32)
        stack = jnp.concatenate(
            [pltpu.roll(inner, DEEP, 1), inner, pltpu.roll(inner, LANES - DEEP, 1)], axis=0
        ).astype(BF16)
        side_part = jnp.dot(taps, stack, preferred_element_type=F32)
        side_left, side_mid, side_right = (side_part[BINS * i : BINS * (i + 1)] for i in range(3))
        side_edge = jnp.where(col == 0, side_right, side_left)
        first = 1 + layer
        pairs = (EXT - 2 - 2 * layer) // 2
        final = layer == layers - 1

        def pair(step, injected):
            row = first + 2 * step
            planes = [active[now, row - 1 + i] for i in range(4)]
            stack = jnp.concatenate(
                [jnp.concatenate(planes[0:3], axis=0), jnp.concatenate(planes[1:4], axis=0)], axis=1
            )
            part = jnp.dot(taps, stack, preferred_element_type=F32)
            for i in range(2):
                here = row + i
                left, mid, right = (
                    part[BINS * k : BINS * (k + 1), LANES * i : LANES * (i + 1)] for k in range(3)
                )
                spot = here * DEEP + near
                moved = pltpu.roll(side_edge, (edge_lane - spot + LANES) % LANES, 1)
                response = mid + jnp.where(lane == 0, 0.0, pltpu.roll(left, 1, 1))
                response = response + jnp.where(lane == LANES - 1, 0.0, pltpu.roll(right, LANES - 1, 1))
                before = joined_ref[here] if layer == 0 else current[here]
                value = before + (response + jnp.where(at_edge, moved, 0.0))
                if final:
                    out_ref[here - DEEP] = value
                else:
                    current[here] = value
                    keep = ((here >= DEEP) | has_above) & ((here < ROWS + DEEP) | has_below)
                    active[later, here] = jnp.where(keep, silu(value), 0.0).astype(BF16)
                    outward = jnp.where(col == 0, left, right)
                    thrown = pltpu.roll(outward, (spot - edge_lane + LANES) % LANES, 1)
                    injected = jnp.where(lane == spot, thrown, injected)
            return injected

        injected = jnp.zeros((BINS, LANES), F32)
        for step in range(pairs):
            injected = pair(step, injected)
            if final and (step + 1) % SENT == 0:
                rows = pl.ds(2 * (step + 1 - SENT), 2 * SENT)
                copy = pltpu.make_async_copy(out_ref.at[rows], out_hbm.at[rows], sems.at[len(leaving)])
                copy.start()
                leaving.append(copy)
        if not final:
            place = lane % DEEP
            from_left = jnp.where((place == 0) & (col == 0), injected, pltpu.roll(side_left, 1, 1))
            from_right = jnp.where((place == DEEP - 1) & (col != 0), injected, pltpu.roll(side_right, LANES - 1, 1))
            side_current = side_current + (side_mid + from_left + from_right)
            side_active[...] = jnp.where(inside, silu(side_current), 0.0).astype(BF16)
    for copy in leaving:
        copy.wait()


def refine(spot, matrix, joined, side):
    vmem = pl.BlockSpec(memory_space=pltpu.VMEM)
    smem = pl.BlockSpec(memory_space=pltpu.SMEM)
    anywhere = pl.BlockSpec(memory_space=pl.ANY)
    flat = (ROWS,) + joined.shape[1:]
    return pl.pallas_call(
        refine_kernel,
        out_shape=jax.ShapeDtypeStruct(flat, F32),
        in_specs=[smem, vmem, vmem, vmem],
        out_specs=anywhere,
        scratch_shapes=[
            pltpu.VMEM(flat, F32),
            pltpu.VMEM(joined.shape, F32),
            pltpu.VMEM((2,) + joined.shape, BF16),
            pltpu.VMEM((BINS, LANES), BF16),
            pltpu.SemaphoreType.DMA((ROWS // (2 * SENT),)),
        ],
        compiler_params=pltpu.CompilerParams(vmem_limit_bytes=16 << 20),
        name="refine",
    )(spot, matrix, joined, side)


def on_device(tsdf_prior, prior_weight, depth_maps, confidence, frustum_tiles, pixel_index, conv_weights):
    row_count = lax.axis_size("row")
    spot = jnp.stack([lax.axis_index("row"), lax.axis_index("col"), jnp.int32(row_count - 1)]).astype(I32)
    readers = frustum_tiles.shape[1]
    both = ("row", "col")
    words = sample(
        pixel_index.reshape(-1, LANES),
        frustum_tiles[0].T,
        depth_maps.reshape(-1, LANES),
        confidence.reshape(-1, LANES),
    )
    width = WIDTH * LANES
    got = lax.all_to_all(words.reshape(readers, 1, width), both, split_axis=0, concat_axis=0, tiled=True)
    def halo(first):
        rows = slice(first, first + DEEP)
        return jnp.concatenate([tsdf_prior[rows], prior_weight[rows]], axis=0).astype(BF16)

    up = [(i, i + 1) for i in range(row_count - 1)]
    down = [(j, i) for i, j in up]
    above = lax.ppermute(halo(ROWS - DEEP), "row", up)
    below = lax.ppermute(halo(0), "row", down)
    layers = conv_weights.shape[0]
    matrix = tap_matrices(conv_weights.reshape(layers, BINS, GROUP * 9))
    above, matrix = lax.optimization_barrier((above, matrix))
    start = (WIDTH - 1) * LANES
    tiles = got[:, 0, start : start + WIDTH - 1]
    places = lax.broadcasted_iota(I32, tiles.shape, 0) * WIDTH + lax.broadcasted_iota(I32, tiles.shape, 1)
    codes = jnp.where(tiles >= 0, tiles * 1024 + places, -1)
    joined, new_weight, edge = join(
        spot,
        codes,
        got.reshape(WIDTH * readers, LANES),
        above,
        below,
        tsdf_prior,
        prior_weight,
    )
    side = lax.ppermute(edge, "col", [(0, 1), (1, 0)])
    refined = refine(spot, matrix, joined, side)
    return refined, new_weight


def solution(mesh):
    placed = (
        P("row", None, "col"),
        P("row", None, "col"),
        P("row", None),
        P("row", None),
        P(("row", "col"), None, None),
        P(("row", "col"), None, None, None),
        P(),
    )
    return jax.shard_map(
        on_device,
        mesh=mesh,
        in_specs=placed,
        out_specs=(P("row", None, "col"), P("row", None, "col")),
        check_vma=False,
    )
```

```python
import jax
import jax.numpy as jnp
from jax import lax
from jax.experimental import pallas as pl
from jax.experimental.pallas import tpu as pltpu
from jax.sharding import PartitionSpec as P

LANES = 128
BINS = 64
ROWS = 32
DEEP = 3
EXT = ROWS + 2 * DEEP
GROUP = 16
AT_ONCE = 4
WIDTH = 5
JOIN_VMEM = 16
SENT = 4
H_SCALE = 1023.0
C_SCALE = 13000.0
F32 = jnp.float32
BF16 = jnp.bfloat16
I32 = jnp.int32


BY_BLOCK = [("v", 0), ("v", 1), ("v", 2), ("v", 3), ("s", 0), ("s", 1), ("s", 2), ("l", 0), ("l", 1), ("l", 2)]
BY_BLOCK += [("v", 4), ("l", 3), ("l", 4), ("l", 5), ("l", 6)]
BY_LANE = [("v", i) for i in range(5)] + [("s", i) for i in range(3)] + [("l", i) for i in range(7)]
REGISTERS = 32
LAG = 8


def along(kind):
    return lax.broadcasted_iota(I32, (8, LANES), 0 if kind == "s" else 1)


def exchange(parts, kind, bit):
    distance = 1 << bit
    if kind == "v":
        parts = list(parts)
        for low in range(REGISTERS):
            if low & distance == 0:
                one, two = parts[low], parts[low | distance]
                parts[low], parts[low | distance] = jnp.minimum(one, two), jnp.maximum(one, two)
        return parts
    axis = 0 if kind == "s" else 1
    size = (8, LANES)[axis]
    upper = (along(kind) & distance) != 0
    result = []
    for part in parts:
        from_low = pltpu.roll(part, distance, axis)
        from_high = from_low if 2 * distance == size else pltpu.roll(part, size - distance, axis)
        result.append(jnp.where(upper, jnp.maximum(part, from_low), jnp.minimum(part, from_high)))
    return result


def turn(parts, places):
    fixed = [bit for kind, bit in places if kind == "v"]
    mask = None
    for kind, bit in places:
        if kind != "v":
            one = -((along(kind) >> bit) & 1)
            mask = one if mask is None else mask ^ one
    result = []
    for register, part in enumerate(parts):
        if sum((register >> bit) & 1 for bit in fixed) % 2:
            part = ~part
        result.append(part if mask is None else part ^ mask)
    return result


def sort_steps(order):
    size = len(order)
    for phase in range(1, size + 1):
        yield "turn", [order[place] for place in (phase - 1, phase) if 0 < place < size and phase + place > 1]
        for place in range(phase - 1, -1, -1):
            yield "exchange", order[place]


def advance(parts, step):
    kind, what = step
    return turn(parts, what) if kind == "turn" else exchange(parts, *what)


def sample_kernel(pixel_ref, wanted_ref, height_hbm, conf_hbm, out_ref, maps, table, blocks, found, edges, bounds, sems):
    copies = [
        pltpu.make_async_copy(height_hbm, maps.at[0], sems.at[0]),
        pltpu.make_async_copy(conf_hbm, maps.at[1], sems.at[1]),
    ]
    for copy in copies:
        copy.start()
    parts = []
    for register in range(REGISTERS):
        pixel = pixel_ref[8 * register : 8 * register + 8, :]
        place = ((along("s") & 1) << 4) + (register >> 1)
        place = place + ((4 * (register & 1) + (along("s") >> 1)) << 5) + (along("l") << 8)
        parts.append(((pixel - 65536) << 15) | place)
    for step in sort_steps(BY_BLOCK):
        parts = advance(parts, step)
    for i, register in enumerate((0, 16, 15, 31)):
        edges[8 * i : 8 * i + 8, :] = parts[register]
    to_scalar = pltpu.make_async_copy(edges, bounds, sems.at[2])
    to_scalar.start()
    for half in range(2):
        turned = jnp.concatenate(parts[16 * half : 16 * half + 16], axis=0).T
        for i in range(16):
            blocks[8 * (2 * i + half) : 8 * (2 * i + half) + 8, :] = turned[8 * i : 8 * i + 8, :]
    for copy in copies:
        copy.wait()
    high = (maps[0] * H_SCALE + 0.5).astype(I32) - 32768
    low = (maps[1] * C_SCALE + 0.5).astype(I32)
    table[...] = (high << 16) | low
    to_scalar.wait()
    chunks = table.shape[0] // 8
    together = 16

    def first_chunk(block):
        return (bounds[8 * (block & 1), 8 * (block >> 1)] >> 25) + 64

    def last_chunk(block):
        return (bounds[23 + 8 * (block & 1), 8 * (block >> 1) + 7] >> 25) + 64

    def walk(index, carry):
        chunk, block = carry
        pending = []
        for _ in range(together):
            rows = pl.ds(pl.multiple_of(block * 8, 8), 8)
            key = blocks[rows, :]
            lane = (key >> 15) & (LANES - 1)
            line = (key >> 22) + 512
            value = jnp.zeros((8, LANES), I32)
            for offset in range(8):
                row = chunk * 8 + offset
                words = jnp.broadcast_to(table[pl.ds(row, 1), :], (8, LANES))
                taken = jnp.take_along_axis(words, lane, axis=1)
                value = jnp.where(line == row, taken, value)
            pending.append((rows, (line >> 3) == chunk, value))
            after = jnp.minimum(block + 1, REGISTERS - 1)
            stay = last_chunk(block) > chunk
            chunk = jnp.where(stay, chunk + 1, first_chunk(after))
            block = jnp.where(stay, block, after)
        for rows, mine, value in pending:
            found[rows, :] = jnp.where(mine, value, found[rows, :])
        return chunk, block

    lax.fori_loop(0, (REGISTERS + chunks) // together, walk, (first_chunk(0), jnp.int32(0)))
    highs, lows = [], []
    for register in range(REGISTERS):
        rows = slice(8 * register, 8 * register + 8)
        place = ((blocks[rows, :] & 32767) - 16384) << 16
        word = found[rows, :]
        highs.append(place | ((word >> 16) & 0xFFFF))
        lows.append(place | (word & 0xFFFF))
    steps = list(sort_steps(BY_LANE))
    for i in range(len(steps) + LAG):
        if i < len(steps):
            highs = advance(highs, steps[i])
        if i >= LAG:
            lows = advance(lows, steps[i - LAG])
    owners = wanted_ref.shape[1]
    blank = jnp.zeros((1, LANES), I32)
    for owner in range(2):
        out_ref[WIDTH * owner + 3 : WIDTH * owner + 4, :] = blank
        out_ref[WIDTH * (owners - 1 - owner) + 2 : WIDTH * (owners - 1 - owner) + 3, :] = blank
    for register in range(REGISTERS):
        slot, owner = register >> 4, 8 * (register & 15)
        word = (highs[register] << 16) | (lows[register] & 0xFFFF)
        out_ref[pl.ds(WIDTH * owner + slot, 8, stride=WIDTH), :] = word
        if slot == 0 and owner == 0:
            out_ref[pl.ds(2, 6, stride=WIDTH), :] = word[2:8]
        elif slot == 0:
            out_ref[pl.ds(WIDTH * (owner - 2) + 2, 8, stride=WIDTH), :] = word
        elif owner == owners - 8:
            out_ref[pl.ds(WIDTH * (owner + 2) + 3, 6, stride=WIDTH), :] = word[0:6]
        else:
            out_ref[pl.ds(WIDTH * (owner + 2) + 3, 8, stride=WIDTH), :] = word
    lane = lax.broadcasted_iota(I32, (1, LANES), 1)
    first, second = wanted_ref[0:1, :], wanted_ref[1:2, :]
    below = pltpu.roll(jnp.broadcast_to(first, (8, LANES)), LANES - 2, 1)[0:1]
    above = pltpu.roll(jnp.broadcast_to(second, (8, LANES)), 2, 1)[0:1]
    tiles = [
        jnp.where(first >= 0, first + DEEP, -1),
        jnp.where(second >= 0, second + DEEP, -1),
        jnp.where((below >= 0) & (below < DEEP) & (lane < owners - 2), below + (ROWS + DEEP), -1),
        jnp.where((above >= ROWS - DEEP) & (lane >= 2), above - (ROWS - DEEP), -1),
    ]
    turned = jnp.concatenate(tiles + [jnp.zeros((LANES - 4, LANES), I32)], axis=0).T
    for owner in range(0, owners, 8):
        out_ref[pl.ds(WIDTH * owner + WIDTH - 1, 8, stride=WIDTH), :] = turned[owner : owner + 8, :]


def sample(pixels, wanted, heights, confidence):
    flat = pltpu.VMEM(pixels.shape, I32)
    return pl.pallas_call(
        sample_kernel,
        out_shape=jax.ShapeDtypeStruct((WIDTH * wanted.shape[1], LANES), I32),
        in_specs=[
            pl.BlockSpec(memory_space=pltpu.VMEM),
            pl.BlockSpec(memory_space=pltpu.VMEM),
            pl.BlockSpec(memory_space=pl.ANY),
            pl.BlockSpec(memory_space=pl.ANY),
        ],
        out_specs=pl.BlockSpec(memory_space=pltpu.VMEM),
        scratch_shapes=[
            pltpu.VMEM((2,) + heights.shape, F32),
            pltpu.VMEM(heights.shape, I32),
            flat,
            flat,
            pltpu.VMEM((32, LANES), I32),
            pltpu.SMEM((32, LANES), I32),
            pltpu.SemaphoreType.DMA((3,)),
        ],
        compiler_params=pltpu.CompilerParams(vmem_limit_bytes=60 << 20),
        name="sample",
    )(pixels, wanted, heights, confidence)


def join_kernel(
    spot_ref, list_ref, words_ref, above_ref, below_ref, prior_hbm, weight_hbm,
    joined_ref, new_hbm, edge_ref,
    order_ref, height, certainty, prior_ref, total, sems,
):
    inner = pl.ds(DEEP, ROWS)
    copies = [
        pltpu.make_async_copy(prior_hbm, prior_ref.at[inner], sems.at[0]),
        pltpu.make_async_copy(weight_hbm, total.at[inner], sems.at[1]),
    ]
    for copy in copies:
        copy.start()
    col = spot_ref[1]
    entries = words_ref.shape[0]
    word = words_ref[...]
    height[0:entries, :] = ((word >> 16) + 32768).astype(F32) * (0.5 / H_SCALE)
    certainty[0:entries, :] = (word & 0xFFFF).astype(F32) * (0.5 / C_SCALE)
    height[entries:, :] = jnp.zeros((8, LANES), F32)
    certainty[entries:, :] = jnp.zeros((8, LANES), F32)
    level = lax.broadcasted_iota(I32, (BINS, LANES), 0).astype(F32) * 0.5

    half = list_ref.shape[0] // 2
    room = order_ref.shape[0] // 2

    def pick(step, counts):
        counts = list(counts)
        codes = [[list_ref[2 * step + i + half * side, slot] for i in range(2) for slot in range(WIDTH - 1)] for side in range(2)]
        for pair in zip(*codes):
            for side in range(2):
                order_ref[room * side + counts[side]] = pair[side]
                counts[side] = counts[side] + (1 + (pair[side] >> 31))
        return tuple(counts)

    counts = lax.fori_loop(0, half // 2, pick, (jnp.int32(0), jnp.int32(0)), unroll=2)
    for side in range(2):
        for i in range(AT_ONCE):
            order_ref[room * side + counts[side] + i] = entries
    for copy in copies:
        copy.wait()
    for row in range(DEEP):
        prior_ref[row] = above_ref[row].astype(F32)
        prior_ref[ROWS + DEEP + row] = below_ref[row].astype(F32)
        total[row] = above_ref[DEEP + row].astype(F32)
        total[ROWS + DEEP + row] = below_ref[DEEP + row].astype(F32)
    for row in range(EXT):
        twice = 2.0 * prior_ref[row]
        prior_ref[row] = twice
        joined_ref[row] = total[row] * twice

    def term(place):
        code = order_ref[place]
        tile = code >> 10
        entry = code & 1023
        twice = prior_ref[tile]
        scaled = height[pl.ds(entry, 1), :] - level
        signed = jnp.clip(scaled, -2.0, 2.0)
        visible = jnp.clip(scaled + 4.0, 0.0, 2.0)
        mismatch = signed - twice
        spread = 1.0 + mismatch * mismatch
        inverse = pl.reciprocal(spread, approx=True)
        observed = (certainty[pl.ds(entry, 1), :] * visible) * inverse
        return tile, observed, observed * signed

    def step(index, carry):
        terms = [term(AT_ONCE * index + i) for i in range(AT_ONCE)]
        for tile, observed, weighted in terms:
            total[tile] += observed
            joined_ref[tile] += weighted
        return carry

    steps = [(count + AT_ONCE - 1) // AT_ONCE for count in counts]

    def either(index, carry):
        return step(jnp.where(index < steps[0], index, index - steps[0] + room // AT_ONCE), carry)

    lax.fori_loop(0, steps[0] + steps[1], either, 0)
    leaving = pltpu.make_async_copy(total.at[inner], new_hbm, sems.at[0])
    leaving.start()
    lane = lax.broadcasted_iota(I32, (BINS, LANES), 1)
    source = jnp.where(col == 0, LANES - DEEP, 0)
    has_above = spot_ref[0] > 0
    has_below = spot_ref[0] < spot_ref[2]
    edge = jnp.zeros((BINS, LANES), F32)
    for row in range(EXT):
        inverse = pl.reciprocal(total[row], approx=True)
        value = (0.5 * joined_ref[row]) * inverse
        if row < DEEP:
            value = jnp.where(has_above, value, 0.0)
        elif row >= ROWS + DEEP:
            value = jnp.where(has_below, value, 0.0)
        joined_ref[row] = value
        start = row * DEEP
        moved = pltpu.roll(value, (start - source + LANES) % LANES, 1)
        edge = jnp.where((lane >= start) & (lane < start + DEEP), moved, edge)
    edge_ref[...] = edge
    leaving.wait()


def join(spot, lists, words, above, below, prior, weight):
    rows, bins, lanes = prior.shape
    tall = (rows + 2 * DEEP, bins, lanes)
    vmem = pl.BlockSpec(memory_space=pltpu.VMEM)
    smem = pl.BlockSpec(memory_space=pltpu.SMEM)
    anywhere = pl.BlockSpec(memory_space=pl.ANY)
    column = pltpu.VMEM((words.shape[0] + 8, LANES), F32)
    return pl.pallas_call(
        join_kernel,
        out_shape=(
            jax.ShapeDtypeStruct(tall, F32),
            jax.ShapeDtypeStruct(prior.shape, F32),
            jax.ShapeDtypeStruct((BINS, LANES), F32),
        ),
        in_specs=[smem, smem, vmem, vmem, vmem, anywhere, anywhere],
        out_specs=(vmem, anywhere, vmem),
        scratch_shapes=[
            pltpu.SMEM(((WIDTH - 1) * lists.shape[0] + 2 * AT_ONCE,), I32),
            column,
            column,
            pltpu.VMEM(tall, F32),
            pltpu.VMEM(tall, F32),
            pltpu.SemaphoreType.DMA((2,)),
        ],
        compiler_params=pltpu.CompilerParams(vmem_limit_bytes=JOIN_VMEM << 20),
        name="join",
    )(spot, lists, words, above, below, prior, weight)


def silu(value):
    half = 0.5 * value
    return half + half * jnp.tanh(half)


def weight_kernel(taps_ref, matrix):
    layers, bins, taps = taps_ref.shape
    tap = lax.broadcasted_iota(I32, (taps, 3 * BINS), 0)
    place = lax.broadcasted_iota(I32, (taps, 3 * BINS), 1)
    out_bin = lax.broadcasted_iota(I32, (BINS, 3 * BINS), 0)
    in_bin = lax.broadcasted_iota(I32, (BINS, 3 * BINS), 1) & (BINS - 1)
    same = (out_bin // GROUP) == (in_bin // GROUP)
    wanted = (place & (GROUP - 1)) * 9 + (place // BINS) * 3
    for offset in range(3):
        chosen = (tap == wanted + offset).astype(F32).astype(BF16)
        for layer in range(layers):
            spread = jnp.dot(taps_ref[layer], chosen, preferred_element_type=F32)
            matrix[layer, BINS * offset : BINS * (offset + 1), :] = jnp.where(same, spread, 0.0).astype(BF16)


def tap_matrices(taps):
    return pl.pallas_call(
        weight_kernel,
        out_shape=jax.ShapeDtypeStruct((taps.shape[0], 3 * BINS, 3 * BINS), BF16),
        in_specs=[pl.BlockSpec(memory_space=pltpu.VMEM)],
        out_specs=pl.BlockSpec(memory_space=pltpu.VMEM),
        compiler_params=pltpu.CompilerParams(vmem_limit_bytes=16 << 20),
        name="tap_matrices",
    )(taps)


def convolve_pair(taps, planes):
    stack = jnp.concatenate([jnp.concatenate(planes[0:3], axis=0), jnp.concatenate(planes[1:4], axis=0)], axis=1)
    part = jnp.dot(taps, stack, preferred_element_type=F32)
    return [
        [part[BINS * k : BINS * (k + 1), LANES * i : LANES * (i + 1)] for k in range(3)] for i in range(2)
    ]


def within(lane, left, mid, right):
    response = mid + jnp.where(lane == 0, 0.0, pltpu.roll(left, 1, 1))
    return response + jnp.where(lane == LANES - 1, 0.0, pltpu.roll(right, LANES - 1, 1))


def geometry(spot_ref):
    col = spot_ref[1]
    lane = lax.broadcasted_iota(I32, (BINS, LANES), 1)
    edge_lane = jnp.where(col == 0, LANES - 1, 0)
    near = jnp.where(col == 0, 0, DEEP - 1)
    return col, lane, edge_lane, near


def outward_edge(col, lane, edge_lane, spot, left, right, injected):
    outward = jnp.where(col == 0, left, right)
    thrown = pltpu.roll(outward, (spot - edge_lane + LANES) % LANES, 1)
    return jnp.where(lane == spot, thrown, injected)


def open_kernel(spot_ref, matrix, joined_ref, partial_ref, injected_ref, active):
    col, lane, edge_lane, near = geometry(spot_ref)
    for row in range(EXT):
        active[row] = silu(joined_ref[row]).astype(BF16)
    partial_ref[0] = joined_ref[0]
    partial_ref[EXT - 1] = joined_ref[EXT - 1]
    injected = jnp.zeros((BINS, LANES), F32)
    for row in range(1, EXT - 1, 2):
        parts = convolve_pair(matrix[0], [active[row - 1 + i] for i in range(4)])
        for i, (left, mid, right) in enumerate(parts):
            partial_ref[row + i] = joined_ref[row + i] + within(lane, left, mid, right)
            injected = outward_edge(col, lane, edge_lane, (row + i) * DEEP + near, left, right, injected)
    injected_ref[...] = injected


def open_layer(spot, matrix, joined):
    vmem = pl.BlockSpec(memory_space=pltpu.VMEM)
    return pl.pallas_call(
        open_kernel,
        out_shape=(
            jax.ShapeDtypeStruct(joined.shape, F32),
            jax.ShapeDtypeStruct((BINS, LANES), F32),
        ),
        in_specs=[pl.BlockSpec(memory_space=pltpu.SMEM), vmem, vmem],
        out_specs=(vmem, vmem),
        scratch_shapes=[pltpu.VMEM(joined.shape, BF16)],
        compiler_params=pltpu.CompilerParams(vmem_limit_bytes=16 << 20),
        cost_estimate=pl.CostEstimate(flops=400_000_000, bytes_accessed=3_000_000, transcendentals=311_296),
        name="open_layer",
    )(spot, matrix, joined)


def refine_kernel(
    spot_ref, matrix, partial_ref, injected_ref, side_ref, out_hbm, out_ref, current, active, side_active, sems
):
    row_index, last_row = spot_ref[0], spot_ref[2]
    col, lane, edge_lane, near = geometry(spot_ref)
    has_above = row_index > 0
    has_below = row_index < last_row
    leaving = []
    inside = ((lane >= DEEP * DEEP) | has_above) & ((lane < (ROWS + DEEP) * DEEP) | has_below)
    at_edge = lane == edge_lane
    place = lane % DEEP

    side_current = side_ref[...]
    side_active[...] = silu(side_current).astype(BF16)

    layers = matrix.shape[0]
    for layer in range(layers):
        now, later = layer % 2, (layer + 1) % 2
        taps = matrix[layer]
        inner = side_active[...].astype(F32)
        stack = jnp.concatenate(
            [pltpu.roll(inner, DEEP, 1), inner, pltpu.roll(inner, LANES - DEEP, 1)], axis=0
        ).astype(BF16)
        side_part = jnp.dot(taps, stack, preferred_element_type=F32)
        side_left, side_mid, side_right = (side_part[BINS * i : BINS * (i + 1)] for i in range(3))
        side_edge = jnp.where(col == 0, side_right, side_left)
        first = 1 + layer
        final = layer == layers - 1

        def inward(row):
            spot = row * DEEP + near
            moved = pltpu.roll(side_edge, (edge_lane - spot + LANES) % LANES, 1)
            return jnp.where(at_edge, moved, 0.0)

        def keep(row, value):
            current[row] = value
            if row < DEEP:
                value = jnp.where(has_above, silu(value), 0.0)
            elif row >= ROWS + DEEP:
                value = jnp.where(has_below, silu(value), 0.0)
            else:
                value = silu(value)
            active[later, row] = value.astype(BF16)

        if layer == 0:
            injected = injected_ref[...]
            for row in range(first, EXT - first):
                keep(row, partial_ref[row] + inward(row))
        else:
            injected = jnp.zeros((BINS, LANES), F32)
            for row in range(first, EXT - first, 2):
                parts = convolve_pair(taps, [active[now, row - 1 + i] for i in range(4)])
                for i, (left, mid, right) in enumerate(parts):
                    here = row + i
                    value = current[here] + (within(lane, left, mid, right) + inward(here))
                    if final:
                        out_ref[here - DEEP] = value
                    else:
                        keep(here, value)
                        injected = outward_edge(col, lane, edge_lane, here * DEEP + near, left, right, injected)
                done = row + 2 - DEEP
                if final and done % (2 * SENT) == 0:
                    rows = pl.ds(done - 2 * SENT, 2 * SENT)
                    copy = pltpu.make_async_copy(out_ref.at[rows], out_hbm.at[rows], sems.at[len(leaving)])
                    copy.start()
                    leaving.append(copy)
        if not final:
            from_left = jnp.where((place == 0) & (col == 0), injected, pltpu.roll(side_left, 1, 1))
            from_right = jnp.where((place == DEEP - 1) & (col != 0), injected, pltpu.roll(side_right, LANES - 1, 1))
            side_current = side_current + (side_mid + from_left + from_right)
            side_active[...] = jnp.where(inside, silu(side_current), 0.0).astype(BF16)
    for copy in leaving:
        copy.wait()


def refine(spot, matrix, partial, injected, side):
    vmem = pl.BlockSpec(memory_space=pltpu.VMEM)
    smem = pl.BlockSpec(memory_space=pltpu.SMEM)
    anywhere = pl.BlockSpec(memory_space=pl.ANY)
    flat = (ROWS,) + partial.shape[1:]
    return pl.pallas_call(
        refine_kernel,
        out_shape=jax.ShapeDtypeStruct(flat, F32),
        in_specs=[smem, vmem, vmem, vmem, vmem],
        out_specs=anywhere,
        scratch_shapes=[
            pltpu.VMEM(flat, F32),
            pltpu.VMEM(partial.shape, F32),
            pltpu.VMEM((2,) + partial.shape, BF16),
            pltpu.VMEM((BINS, LANES), BF16),
            pltpu.SemaphoreType.DMA((ROWS // (2 * SENT),)),
        ],
        compiler_params=pltpu.CompilerParams(vmem_limit_bytes=16 << 20),
        name="refine",
    )(spot, matrix, partial, injected, side)


def on_device(tsdf_prior, prior_weight, depth_maps, confidence, frustum_tiles, pixel_index, conv_weights):
    row_count = lax.axis_size("row")
    spot = jnp.stack([lax.axis_index("row"), lax.axis_index("col"), jnp.int32(row_count - 1)]).astype(I32)
    readers = frustum_tiles.shape[1]
    both = ("row", "col")
    words = sample(
        pixel_index.reshape(-1, LANES),
        frustum_tiles[0].T,
        depth_maps.reshape(-1, LANES),
        confidence.reshape(-1, LANES),
    )
    width = WIDTH * LANES
    got = lax.all_to_all(words.reshape(readers, 1, width), both, split_axis=0, concat_axis=0, tiled=True)
    def halo(first):
        rows = slice(first, first + DEEP)
        return jnp.concatenate([tsdf_prior[rows], prior_weight[rows]], axis=0).astype(BF16)

    up = [(i, i + 1) for i in range(row_count - 1)]
    down = [(j, i) for i, j in up]
    above = lax.ppermute(halo(ROWS - DEEP), "row", up)
    below = lax.ppermute(halo(0), "row", down)
    layers = conv_weights.shape[0]
    matrix = tap_matrices(conv_weights.reshape(layers, BINS, GROUP * 9))
    above, matrix = lax.optimization_barrier((above, matrix))
    start = (WIDTH - 1) * LANES
    tiles = got[:, 0, start : start + WIDTH - 1]
    places = lax.broadcasted_iota(I32, tiles.shape, 0) * WIDTH + lax.broadcasted_iota(I32, tiles.shape, 1)
    codes = jnp.where(tiles >= 0, tiles * 1024 + places, -1)
    joined, new_weight, edge = join(
        spot,
        codes,
        got.reshape(WIDTH * readers, LANES),
        above,
        below,
        tsdf_prior,
        prior_weight,
    )
    side = lax.ppermute(edge, "col", [(0, 1), (1, 0)])
    partial, injected = open_layer(spot, matrix, joined)
    refined = refine(spot, matrix, partial, injected, side)
    return refined, new_weight


def solution(mesh):
    placed = (
        P("row", None, "col"),
        P("row", None, "col"),
        P("row", None),
        P("row", None),
        P(("row", "col"), None, None),
        P(("row", "col"), None, None, None),
        P(),
    )
    return jax.shard_map(
        on_device,
        mesh=mesh,
        in_specs=placed,
        out_specs=(P("row", None, "col"), P("row", None, "col")),
        check_vma=False,
    )
```

```python
import jax
import jax.numpy as jnp
from jax import lax
from jax.experimental import pallas as pl
from jax.experimental.pallas import tpu as pltpu
from jax.sharding import PartitionSpec as P

LANES = 128
BINS = 64
ROWS = 32
DEEP = 3
EXT = ROWS + 2 * DEEP
GROUP = 16
AT_ONCE = 4
WIDTH = 5
JOIN_VMEM = 16
SENT = 4
H_SCALE = 1023.0
C_SCALE = 13000.0
F32 = jnp.float32
BF16 = jnp.bfloat16
I32 = jnp.int32


BY_BLOCK = [("v", 0), ("v", 1), ("v", 2), ("v", 3), ("s", 0), ("s", 1), ("s", 2), ("l", 0), ("l", 1), ("l", 2)]
BY_BLOCK += [("v", 4), ("l", 3), ("l", 4), ("l", 5), ("l", 6)]
BY_LANE = [("v", i) for i in range(5)] + [("s", i) for i in range(3)] + [("l", i) for i in range(7)]
REGISTERS = 32
LAG = 8


def along(kind):
    return lax.broadcasted_iota(I32, (8, LANES), 0 if kind == "s" else 1)


def exchange(parts, kind, bit):
    distance = 1 << bit
    if kind == "v":
        parts = list(parts)
        for low in range(REGISTERS):
            if low & distance == 0:
                one, two = parts[low], parts[low | distance]
                parts[low], parts[low | distance] = jnp.minimum(one, two), jnp.maximum(one, two)
        return parts
    axis = 0 if kind == "s" else 1
    size = (8, LANES)[axis]
    upper = (along(kind) & distance) != 0
    result = []
    for part in parts:
        from_low = pltpu.roll(part, distance, axis)
        from_high = from_low if 2 * distance == size else pltpu.roll(part, size - distance, axis)
        result.append(jnp.where(upper, jnp.maximum(part, from_low), jnp.minimum(part, from_high)))
    return result


def turn(parts, places):
    fixed = [bit for kind, bit in places if kind == "v"]
    mask = None
    for kind, bit in places:
        if kind != "v":
            one = -((along(kind) >> bit) & 1)
            mask = one if mask is None else mask ^ one
    result = []
    for register, part in enumerate(parts):
        if sum((register >> bit) & 1 for bit in fixed) % 2:
            part = ~part
        result.append(part if mask is None else part ^ mask)
    return result


def sort_steps(order):
    size = len(order)
    for phase in range(1, size + 1):
        yield "turn", [order[place] for place in (phase - 1, phase) if 0 < place < size and phase + place > 1]
        for place in range(phase - 1, -1, -1):
            yield "exchange", order[place]


def advance(parts, step):
    kind, what = step
    return turn(parts, what) if kind == "turn" else exchange(parts, *what)


def sample_kernel(pixel_ref, wanted_ref, height_hbm, conf_hbm, out_ref, maps, table, blocks, found, edges, bounds, sems):
    copies = [
        pltpu.make_async_copy(height_hbm, maps.at[0], sems.at[0]),
        pltpu.make_async_copy(conf_hbm, maps.at[1], sems.at[1]),
    ]
    for copy in copies:
        copy.start()
    parts = []
    for register in range(REGISTERS):
        pixel = pixel_ref[8 * register : 8 * register + 8, :]
        place = ((along("s") & 1) << 4) + (register >> 1)
        place = place + ((4 * (register & 1) + (along("s") >> 1)) << 5) + (along("l") << 8)
        parts.append(((pixel - 65536) << 15) | place)
    for step in sort_steps(BY_BLOCK):
        parts = advance(parts, step)
    for i, register in enumerate((0, 16, 15, 31)):
        edges[8 * i : 8 * i + 8, :] = parts[register]
    to_scalar = pltpu.make_async_copy(edges, bounds, sems.at[2])
    to_scalar.start()
    for half in range(2):
        turned = jnp.concatenate(parts[16 * half : 16 * half + 16], axis=0).T
        for i in range(16):
            blocks[8 * (2 * i + half) : 8 * (2 * i + half) + 8, :] = turned[8 * i : 8 * i + 8, :]
    for copy in copies:
        copy.wait()
    high = (maps[0] * H_SCALE + 0.5).astype(I32) - 32768
    low = (maps[1] * C_SCALE + 0.5).astype(I32)
    table[...] = (high << 16) | low
    to_scalar.wait()
    chunks = table.shape[0] // 8
    together = 16

    def first_chunk(block):
        return (bounds[8 * (block & 1), 8 * (block >> 1)] >> 25) + 64

    def last_chunk(block):
        return (bounds[23 + 8 * (block & 1), 8 * (block >> 1) + 7] >> 25) + 64

    def walk(index, carry):
        chunk, block = carry
        pending = []
        for _ in range(together):
            rows = pl.ds(pl.multiple_of(block * 8, 8), 8)
            key = blocks[rows, :]
            lane = (key >> 15) & (LANES - 1)
            line = (key >> 22) + 512
            value = jnp.zeros((8, LANES), I32)
            for offset in range(8):
                row = chunk * 8 + offset
                words = jnp.broadcast_to(table[pl.ds(row, 1), :], (8, LANES))
                taken = jnp.take_along_axis(words, lane, axis=1)
                value = jnp.where(line == row, taken, value)
            pending.append((rows, (line >> 3) == chunk, value))
            after = jnp.minimum(block + 1, REGISTERS - 1)
            stay = last_chunk(block) > chunk
            chunk = jnp.where(stay, chunk + 1, first_chunk(after))
            block = jnp.where(stay, block, after)
        for rows, mine, value in pending:
            found[rows, :] = jnp.where(mine, value, found[rows, :])
        return chunk, block

    lax.fori_loop(0, (REGISTERS + chunks) // together, walk, (first_chunk(0), jnp.int32(0)))
    highs, lows = [], []
    for register in range(REGISTERS):
        rows = slice(8 * register, 8 * register + 8)
        place = ((blocks[rows, :] & 32767) - 16384) << 16
        word = found[rows, :]
        highs.append(place | ((word >> 16) & 0xFFFF))
        lows.append(place | (word & 0xFFFF))
    steps = list(sort_steps(BY_LANE))
    for i in range(len(steps) + LAG):
        if i < len(steps):
            highs = advance(highs, steps[i])
        if i >= LAG:
            lows = advance(lows, steps[i - LAG])
    owners = wanted_ref.shape[1]
    blank = jnp.zeros((1, LANES), I32)
    for owner in range(2):
        out_ref[WIDTH * owner + 3 : WIDTH * owner + 4, :] = blank
        out_ref[WIDTH * (owners - 1 - owner) + 2 : WIDTH * (owners - 1 - owner) + 3, :] = blank
    for register in range(REGISTERS):
        slot, owner = register >> 4, 8 * (register & 15)
        word = (highs[register] << 16) | (lows[register] & 0xFFFF)
        out_ref[pl.ds(WIDTH * owner + slot, 8, stride=WIDTH), :] = word
        if slot == 0 and owner == 0:
            out_ref[pl.ds(2, 6, stride=WIDTH), :] = word[2:8]
        elif slot == 0:
            out_ref[pl.ds(WIDTH * (owner - 2) + 2, 8, stride=WIDTH), :] = word
        elif owner == owners - 8:
            out_ref[pl.ds(WIDTH * (owner + 2) + 3, 6, stride=WIDTH), :] = word[0:6]
        else:
            out_ref[pl.ds(WIDTH * (owner + 2) + 3, 8, stride=WIDTH), :] = word
    lane = lax.broadcasted_iota(I32, (1, LANES), 1)
    first, second = wanted_ref[0:1, :], wanted_ref[1:2, :]
    below = pltpu.roll(jnp.broadcast_to(first, (8, LANES)), LANES - 2, 1)[0:1]
    above = pltpu.roll(jnp.broadcast_to(second, (8, LANES)), 2, 1)[0:1]
    tiles = [
        jnp.where(first >= 0, first + DEEP, -1),
        jnp.where(second >= 0, second + DEEP, -1),
        jnp.where((below >= 0) & (below < DEEP) & (lane < owners - 2), below + (ROWS + DEEP), -1),
        jnp.where((above >= ROWS - DEEP) & (lane >= 2), above - (ROWS - DEEP), -1),
    ]
    turned = jnp.concatenate(tiles + [jnp.zeros((LANES - 4, LANES), I32)], axis=0).T
    for owner in range(0, owners, 8):
        out_ref[pl.ds(WIDTH * owner + WIDTH - 1, 8, stride=WIDTH), :] = turned[owner : owner + 8, :]


def sample(pixels, wanted, heights, confidence):
    flat = pltpu.VMEM(pixels.shape, I32)
    return pl.pallas_call(
        sample_kernel,
        out_shape=jax.ShapeDtypeStruct((WIDTH * wanted.shape[1], LANES), I32),
        in_specs=[
            pl.BlockSpec(memory_space=pltpu.VMEM),
            pl.BlockSpec(memory_space=pltpu.VMEM),
            pl.BlockSpec(memory_space=pl.ANY),
            pl.BlockSpec(memory_space=pl.ANY),
        ],
        out_specs=pl.BlockSpec(memory_space=pltpu.VMEM),
        scratch_shapes=[
            pltpu.VMEM((2,) + heights.shape, F32),
            pltpu.VMEM(heights.shape, I32),
            flat,
            flat,
            pltpu.VMEM((32, LANES), I32),
            pltpu.SMEM((32, LANES), I32),
            pltpu.SemaphoreType.DMA((3,)),
        ],
        compiler_params=pltpu.CompilerParams(vmem_limit_bytes=60 << 20),
        name="sample",
    )(pixels, wanted, heights, confidence)


def join_kernel(
    spot_ref, list_ref, words_ref, above_ref, below_ref, prior_hbm, weight_hbm,
    joined_ref, new_hbm, edge_ref,
    order_ref, height, certainty, prior_ref, total, sems,
):
    inner = pl.ds(DEEP, ROWS)
    copies = [
        pltpu.make_async_copy(prior_hbm, prior_ref.at[inner], sems.at[0]),
        pltpu.make_async_copy(weight_hbm, total.at[inner], sems.at[1]),
    ]
    for copy in copies:
        copy.start()
    col = spot_ref[1]
    entries = words_ref.shape[0]
    word = words_ref[...]
    height[0:entries, :] = ((word >> 16) + 32768).astype(F32) * (0.5 / H_SCALE)
    certainty[0:entries, :] = (word & 0xFFFF).astype(F32) * (0.5 / C_SCALE)
    height[entries:, :] = jnp.zeros((8, LANES), F32)
    certainty[entries:, :] = jnp.zeros((8, LANES), F32)
    level = lax.broadcasted_iota(I32, (BINS, LANES), 0).astype(F32) * 0.5

    half = list_ref.shape[0] // 2
    room = order_ref.shape[0] // 2

    def pick(step, counts):
        counts = list(counts)
        codes = [[list_ref[2 * step + i + half * side, slot] for i in range(2) for slot in range(WIDTH - 1)] for side in range(2)]
        for pair in zip(*codes):
            for side in range(2):
                order_ref[room * side + counts[side]] = pair[side]
                counts[side] = counts[side] + (1 + (pair[side] >> 31))
        return tuple(counts)

    counts = lax.fori_loop(0, half // 2, pick, (jnp.int32(0), jnp.int32(0)), unroll=8)
    for side in range(2):
        for i in range(AT_ONCE):
            order_ref[room * side + counts[side] + i] = entries
    for copy in copies:
        copy.wait()
    for row in range(DEEP):
        prior_ref[row] = above_ref[row].astype(F32)
        prior_ref[ROWS + DEEP + row] = below_ref[row].astype(F32)
        total[row] = above_ref[DEEP + row].astype(F32)
        total[ROWS + DEEP + row] = below_ref[DEEP + row].astype(F32)
    for row in range(EXT):
        twice = 2.0 * prior_ref[row]
        prior_ref[row] = twice
        joined_ref[row] = total[row] * twice

    def term(place):
        code = order_ref[place]
        tile = code >> 10
        entry = code & 1023
        twice = prior_ref[tile]
        scaled = height[pl.ds(entry, 1), :] - level
        signed = jnp.clip(scaled, -2.0, 2.0)
        visible = jnp.clip(scaled + 4.0, 0.0, 2.0)
        mismatch = signed - twice
        spread = 1.0 + mismatch * mismatch
        inverse = pl.reciprocal(spread, approx=True)
        observed = (certainty[pl.ds(entry, 1), :] * visible) * inverse
        return tile, observed, observed * signed

    def step(index, carry):
        terms = [term(AT_ONCE * index + i) for i in range(AT_ONCE)]
        for tile, observed, weighted in terms:
            total[tile] += observed
            joined_ref[tile] += weighted
        return carry

    steps = [(count + AT_ONCE - 1) // AT_ONCE for count in counts]

    def either(index, carry):
        return step(jnp.where(index < steps[0], index, index - steps[0] + room // AT_ONCE), carry)

    lax.fori_loop(0, steps[0] + steps[1], either, 0)
    leaving = pltpu.make_async_copy(total.at[inner], new_hbm, sems.at[0])
    leaving.start()
    lane = lax.broadcasted_iota(I32, (BINS, LANES), 1)
    source = jnp.where(col == 0, LANES - DEEP, 0)
    has_above = spot_ref[0] > 0
    has_below = spot_ref[0] < spot_ref[2]
    edge = jnp.zeros((BINS, LANES), F32)
    for row in range(EXT):
        inverse = pl.reciprocal(total[row], approx=True)
        value = (0.5 * joined_ref[row]) * inverse
        if row < DEEP:
            value = jnp.where(has_above, value, 0.0)
        elif row >= ROWS + DEEP:
            value = jnp.where(has_below, value, 0.0)
        joined_ref[row] = value
        start = row * DEEP
        moved = pltpu.roll(value, (start - source + LANES) % LANES, 1)
        edge = jnp.where((lane >= start) & (lane < start + DEEP), moved, edge)
    edge_ref[...] = edge
    leaving.wait()


def join(spot, lists, words, above, below, prior, weight):
    rows, bins, lanes = prior.shape
    tall = (rows + 2 * DEEP, bins, lanes)
    vmem = pl.BlockSpec(memory_space=pltpu.VMEM)
    smem = pl.BlockSpec(memory_space=pltpu.SMEM)
    anywhere = pl.BlockSpec(memory_space=pl.ANY)
    column = pltpu.VMEM((words.shape[0] + 8, LANES), F32)
    return pl.pallas_call(
        join_kernel,
        out_shape=(
            jax.ShapeDtypeStruct(tall, F32),
            jax.ShapeDtypeStruct(prior.shape, F32),
            jax.ShapeDtypeStruct((BINS, LANES), F32),
        ),
        in_specs=[smem, smem, vmem, vmem, vmem, anywhere, anywhere],
        out_specs=(vmem, anywhere, vmem),
        scratch_shapes=[
            pltpu.SMEM(((WIDTH - 1) * lists.shape[0] + 2 * AT_ONCE,), I32),
            column,
            column,
            pltpu.VMEM(tall, F32),
            pltpu.VMEM(tall, F32),
            pltpu.SemaphoreType.DMA((2,)),
        ],
        compiler_params=pltpu.CompilerParams(vmem_limit_bytes=JOIN_VMEM << 20),
        name="join",
    )(spot, lists, words, above, below, prior, weight)


def silu(value):
    half = 0.5 * value
    return half + half * jnp.tanh(half)


def weight_kernel(taps_ref, matrix):
    layers, bins, taps = taps_ref.shape
    tap = lax.broadcasted_iota(I32, (taps, 3 * BINS), 0)
    place = lax.broadcasted_iota(I32, (taps, 3 * BINS), 1)
    out_bin = lax.broadcasted_iota(I32, (BINS, 3 * BINS), 0)
    in_bin = lax.broadcasted_iota(I32, (BINS, 3 * BINS), 1) & (BINS - 1)
    same = (out_bin // GROUP) == (in_bin // GROUP)
    wanted = (place & (GROUP - 1)) * 9 + (place // BINS) * 3
    for offset in range(3):
        chosen = (tap == wanted + offset).astype(F32).astype(BF16)
        for layer in range(layers):
            spread = jnp.dot(taps_ref[layer], chosen, preferred_element_type=F32)
            matrix[layer, BINS * offset : BINS * (offset + 1), :] = jnp.where(same, spread, 0.0).astype(BF16)


def tap_matrices(taps):
    return pl.pallas_call(
        weight_kernel,
        out_shape=jax.ShapeDtypeStruct((taps.shape[0], 3 * BINS, 3 * BINS), BF16),
        in_specs=[pl.BlockSpec(memory_space=pltpu.VMEM)],
        out_specs=pl.BlockSpec(memory_space=pltpu.VMEM),
        compiler_params=pltpu.CompilerParams(vmem_limit_bytes=16 << 20),
        name="tap_matrices",
    )(taps)


def convolve_pair(taps, planes):
    stack = jnp.concatenate([jnp.concatenate(planes[0:3], axis=0), jnp.concatenate(planes[1:4], axis=0)], axis=1)
    part = jnp.dot(taps, stack, preferred_element_type=F32)
    return [
        [part[BINS * k : BINS * (k + 1), LANES * i : LANES * (i + 1)] for k in range(3)] for i in range(2)
    ]


def within(lane, left, mid, right):
    response = mid + jnp.where(lane == 0, 0.0, pltpu.roll(left, 1, 1))
    return response + jnp.where(lane == LANES - 1, 0.0, pltpu.roll(right, LANES - 1, 1))


def geometry(spot_ref):
    col = spot_ref[1]
    lane = lax.broadcasted_iota(I32, (BINS, LANES), 1)
    edge_lane = jnp.where(col == 0, LANES - 1, 0)
    near = jnp.where(col == 0, 0, DEEP - 1)
    return col, lane, edge_lane, near


def outward_edge(col, lane, edge_lane, spot, left, right, injected):
    outward = jnp.where(col == 0, left, right)
    thrown = pltpu.roll(outward, (spot - edge_lane + LANES) % LANES, 1)
    return jnp.where(lane == spot, thrown, injected)


def open_kernel(spot_ref, matrix, joined_ref, partial_ref, injected_ref, active):
    col, lane, edge_lane, near = geometry(spot_ref)
    for row in range(EXT):
        active[row] = silu(joined_ref[row]).astype(BF16)
    partial_ref[0] = joined_ref[0]
    partial_ref[EXT - 1] = joined_ref[EXT - 1]
    injected = jnp.zeros((BINS, LANES), F32)
    for row in range(1, EXT - 1, 2):
        parts = convolve_pair(matrix[0], [active[row - 1 + i] for i in range(4)])
        for i, (left, mid, right) in enumerate(parts):
            partial_ref[row + i] = joined_ref[row + i] + within(lane, left, mid, right)
            injected = outward_edge(col, lane, edge_lane, (row + i) * DEEP + near, left, right, injected)
    injected_ref[...] = injected


def open_layer(spot, matrix, joined):
    vmem = pl.BlockSpec(memory_space=pltpu.VMEM)
    return pl.pallas_call(
        open_kernel,
        out_shape=(
            jax.ShapeDtypeStruct(joined.shape, F32),
            jax.ShapeDtypeStruct((BINS, LANES), F32),
        ),
        in_specs=[pl.BlockSpec(memory_space=pltpu.SMEM), vmem, vmem],
        out_specs=(vmem, vmem),
        scratch_shapes=[pltpu.VMEM(joined.shape, BF16)],
        compiler_params=pltpu.CompilerParams(vmem_limit_bytes=16 << 20),
        cost_estimate=pl.CostEstimate(flops=400_000_000, bytes_accessed=3_000_000, transcendentals=311_296),
        name="open_layer",
    )(spot, matrix, joined)


def refine_kernel(
    spot_ref, matrix, partial_ref, injected_ref, side_ref, out_hbm, out_ref, current, active, side_active, sems
):
    row_index, last_row = spot_ref[0], spot_ref[2]
    col, lane, edge_lane, near = geometry(spot_ref)
    has_above = row_index > 0
    has_below = row_index < last_row
    leaving = []
    inside = ((lane >= DEEP * DEEP) | has_above) & ((lane < (ROWS + DEEP) * DEEP) | has_below)
    at_edge = lane == edge_lane
    place = lane % DEEP

    side_current = side_ref[...]
    side_active[...] = silu(side_current).astype(BF16)

    layers = matrix.shape[0]
    for layer in range(layers):
        now, later = layer % 2, (layer + 1) % 2
        taps = matrix[layer]
        inner = side_active[...].astype(F32)
        stack = jnp.concatenate(
            [pltpu.roll(inner, DEEP, 1), inner, pltpu.roll(inner, LANES - DEEP, 1)], axis=0
        ).astype(BF16)
        side_part = jnp.dot(taps, stack, preferred_element_type=F32)
        side_left, side_mid, side_right = (side_part[BINS * i : BINS * (i + 1)] for i in range(3))
        side_edge = jnp.where(col == 0, side_right, side_left)
        first = 1 + layer
        final = layer == layers - 1

        def inward(row):
            spot = row * DEEP + near
            moved = pltpu.roll(side_edge, (edge_lane - spot + LANES) % LANES, 1)
            return jnp.where(at_edge, moved, 0.0)

        def keep(row, value):
            current[row] = value
            if row < DEEP:
                value = jnp.where(has_above, silu(value), 0.0)
            elif row >= ROWS + DEEP:
                value = jnp.where(has_below, silu(value), 0.0)
            else:
                value = silu(value)
            active[later, row] = value.astype(BF16)

        if layer == 0:
            injected = injected_ref[...]
            for row in range(first, EXT - first):
                keep(row, partial_ref[row] + inward(row))
        else:
            injected = jnp.zeros((BINS, LANES), F32)
            for row in range(first, EXT - first, 2):
                parts = convolve_pair(taps, [active[now, row - 1 + i] for i in range(4)])
                for i, (left, mid, right) in enumerate(parts):
                    here = row + i
                    value = current[here] + (within(lane, left, mid, right) + inward(here))
                    if final:
                        out_ref[here - DEEP] = value
                    else:
                        keep(here, value)
                        injected = outward_edge(col, lane, edge_lane, here * DEEP + near, left, right, injected)
                done = row + 2 - DEEP
                if final and done % (2 * SENT) == 0:
                    rows = pl.ds(done - 2 * SENT, 2 * SENT)
                    copy = pltpu.make_async_copy(out_ref.at[rows], out_hbm.at[rows], sems.at[len(leaving)])
                    copy.start()
                    leaving.append(copy)
        if not final:
            from_left = jnp.where((place == 0) & (col == 0), injected, pltpu.roll(side_left, 1, 1))
            from_right = jnp.where((place == DEEP - 1) & (col != 0), injected, pltpu.roll(side_right, LANES - 1, 1))
            side_current = side_current + (side_mid + from_left + from_right)
            side_active[...] = jnp.where(inside, silu(side_current), 0.0).astype(BF16)
    for copy in leaving:
        copy.wait()


def refine(spot, matrix, partial, injected, side):
    vmem = pl.BlockSpec(memory_space=pltpu.VMEM)
    smem = pl.BlockSpec(memory_space=pltpu.SMEM)
    anywhere = pl.BlockSpec(memory_space=pl.ANY)
    flat = (ROWS,) + partial.shape[1:]
    return pl.pallas_call(
        refine_kernel,
        out_shape=jax.ShapeDtypeStruct(flat, F32),
        in_specs=[smem, vmem, vmem, vmem, vmem],
        out_specs=anywhere,
        scratch_shapes=[
            pltpu.VMEM(flat, F32),
            pltpu.VMEM(partial.shape, F32),
            pltpu.VMEM((2,) + partial.shape, BF16),
            pltpu.VMEM((BINS, LANES), BF16),
            pltpu.SemaphoreType.DMA((ROWS // (2 * SENT),)),
        ],
        compiler_params=pltpu.CompilerParams(vmem_limit_bytes=16 << 20),
        name="refine",
    )(spot, matrix, partial, injected, side)


def on_device(tsdf_prior, prior_weight, depth_maps, confidence, frustum_tiles, pixel_index, conv_weights):
    row_count = lax.axis_size("row")
    spot = jnp.stack([lax.axis_index("row"), lax.axis_index("col"), jnp.int32(row_count - 1)]).astype(I32)
    readers = frustum_tiles.shape[1]
    both = ("row", "col")
    words = sample(
        pixel_index.reshape(-1, LANES),
        frustum_tiles[0].T,
        depth_maps.reshape(-1, LANES),
        confidence.reshape(-1, LANES),
    )
    width = WIDTH * LANES
    got = lax.all_to_all(words.reshape(readers, 1, width), both, split_axis=0, concat_axis=0, tiled=True)
    def halo(first):
        rows = slice(first, first + DEEP)
        return jnp.concatenate([tsdf_prior[rows], prior_weight[rows]], axis=0).astype(BF16)

    up = [(i, i + 1) for i in range(row_count - 1)]
    down = [(j, i) for i, j in up]
    above = lax.ppermute(halo(ROWS - DEEP), "row", up)
    below = lax.ppermute(halo(0), "row", down)
    layers = conv_weights.shape[0]
    matrix = tap_matrices(conv_weights.reshape(layers, BINS, GROUP * 9))
    above, matrix = lax.optimization_barrier((above, matrix))
    start = (WIDTH - 1) * LANES
    tiles = got[:, 0, start : start + WIDTH - 1]
    places = lax.broadcasted_iota(I32, tiles.shape, 0) * WIDTH + lax.broadcasted_iota(I32, tiles.shape, 1)
    codes = jnp.where(tiles >= 0, tiles * 1024 + places, -1)
    joined, new_weight, edge = join(
        spot,
        codes,
        got.reshape(WIDTH * readers, LANES),
        above,
        below,
        tsdf_prior,
        prior_weight,
    )
    side = lax.ppermute(edge, "col", [(0, 1), (1, 0)])
    partial, injected = open_layer(spot, matrix, joined)
    refined = refine(spot, matrix, partial, injected, side)
    return refined, new_weight


def solution(mesh):
    placed = (
        P("row", None, "col"),
        P("row", None, "col"),
        P("row", None),
        P("row", None),
        P(("row", "col"), None, None),
        P(("row", "col"), None, None, None),
        P(),
    )
    return jax.shard_map(
        on_device,
        mesh=mesh,
        in_specs=placed,
        out_specs=(P("row", None, "col"), P("row", None, "col")),
        check_vma=False,
    )
```
